512 devices in a mesh: dp: 64 (over y, z), seq: 8 (over x, core).
Axes of the slice: x: 4, y: 4, z: 16, core: 2. Of those that a mesh axis runs over, the one named last changes fastest.
Arguments:
- queries: bfloat16 [131072, 768], P(('dp', 'seq')), may hold values from -160 to 160
- keys: bfloat16 [131072, 768], P(('dp', 'seq')), may hold values from -4 to 4
- values: bfloat16 [131072, 768], P(('dp', 'seq')), may hold values from -6 to 6
- out_grad: bfloat16 [131072, 768], P(('dp', 'seq')), may hold values from -24 to 24
- out_weight: bfloat16 [768, 768], replicated, may hold values from -0.21875 to 0.21875
- slide_lengths: int32 [64, 4], P('dp'), may hold values from 1 to 1024, 2048 in all within a row
Outputs:
- query_grad: bfloat16 [131072, 768], P(('dp', 'seq'))
- key_grad: bfloat16 [131072, 768], P(('dp', 'seq'))
- value_grad: bfloat16 [131072, 768], P(('dp', 'seq'))
- weight_grad: float32 [768, 768], P('dp', 'seq')
The draws below stay inside these ranges and needn't reach their ends.
Inputs may be any that keep to these rules, and one draw needn't show every extreme that they name: `slide_lengths`: the 4 lengths of a group sum to 2048; the longest of each group is exactly 1024.
All inputs are finite; a program needn't handle non-finite values.
Results may differ from the reference program's by a relative error of at most 0.023.
Values may be sent and summed in bfloat16 or wider, within the bound.
A program may use at most 64 MiB of HBM per device.

```python
import math
import jax
import jax.numpy as jnp
import numpy as np
from jax import lax

D = 768
NHEAD = 16
DH = 48
SEG = 256
SLIDES = 4
GROUP_LEN = 2048
DILATION = 8
TOKENS = 131072
N_DP = 64


def shared_rows(key):
    base = jnp.clip(jax.random.normal(key, (TOKENS, D), jnp.float32), -4.0, 4.0)
    return base


def draw_keys(key, part):
    base = shared_rows(key)
    return base.astype(jnp.bfloat16)


def draw_queries(key, part):
    key = jax.random.fold_in(key, 2)
    own = jnp.clip(jax.random.normal(key, (TOKENS, D), jnp.float32), -4.0, 4.0)
    return own.astype(jnp.bfloat16)


def raised(drawn, key, source, target, blocks, factor):
    owner, partner = [(jnp.arange(drawn.shape[position]) // (drawn.shape[position] // blocks)).reshape([-1 if axis == position else 1 for axis in range(drawn.ndim)]) for position in (source, target)]
    chosen = jax.random.permutation(key, blocks)[partner]
    strong = (owner == chosen) | (owner == (partner + blocks // 2) % blocks)
    return jnp.where(strong, factor * drawn, drawn)


def block_levels(stream_key, dims, pieces, least, top_value):
    factor_of, own = 1.0, jax.random.fold_in(stream_key, 6)
    for position, parts in pieces:
        steps = jnp.exp(jax.random.uniform(jax.random.fold_in(own, position), (parts,), jnp.float32, least / len(pieces), top_value / len(pieces)))
        factor_of = factor_of * jnp.repeat(steps, dims[position] // parts).reshape([-1 if axis == position else 1 for axis in range(len(dims))])
    return factor_of


def profile(count, total, reach, skew):
    weights = [(1 << 20) // math.isqrt(standing ** skew) + 1 for standing in range(2, count + 1)]
    surplus, counts = total - reach - (count - 1), [1] * (count - 1)
    while surplus > 0:
        free = [i for i in range(count - 1) if counts[i] < reach]
        pool, remaining = sum([weights[i] for i in free]), surplus
        for i in free:
            more = min(reach - counts[i], max(1, remaining * weights[i] // pool), surplus)
            counts[i] = counts[i] + more
            surplus = surplus - more
    return np.array([reach] + counts)


def ragged(rng, number_of, total, most, skew):
    if number_of == 2:
        one = jax.random.randint(rng, (), max(1, total - most), min(most, total - 1) + 1)
        return jnp.stack([one, total - one])
    sizes = jnp.asarray(profile(number_of, total, most, skew), jnp.int32)
    couples = (number_of - 1) // 2
    giver, sink = sizes[1:1 + 2 * couples:2], sizes[2:2 + 2 * couples:2]
    margin = jnp.minimum(giver - 1, most - sink)
    moved = jax.random.randint(jax.random.fold_in(rng, 1), (couples,), 0, 1 << 20) % (margin + 1)
    sizes = sizes.at[1:1 + 2 * couples:2].set(giver - moved).at[2:2 + 2 * couples:2].set(sink + moved)
    return sizes[jax.random.permutation(jax.random.fold_in(rng, 2), number_of)]


def scatter_about(rng, extent, width, reach, pieces=(), kind=jnp.bfloat16):
    level = block_levels(rng, extent, pieces, -0.22, 0.18) if pieces else 1.0
    entries = jax.random.normal(rng, extent, jnp.float32) * width * level
    return jnp.minimum(jnp.maximum(entries, -reach), reach).astype(kind)


def noise_with(stream_key, shape, scale, limit, pieces, heavy, kind=jnp.bfloat16):
    entries = scale * jax.random.normal(stream_key, shape, jnp.float32)
    if pieces:
        entries = entries * block_levels(stream_key, shape, pieces, -0.22, 0.18)
    return jnp.clip(raised(entries, jax.random.fold_in(stream_key, 3), *heavy), -limit, limit).astype(kind)


def setup_inputs(seed: int = 0) -> dict:
    arg_keys = jax.random.split(jax.random.key(seed), 7)
    queries = draw_queries(jax.random.fold_in(arg_keys[6], 71), 0)
    keys = draw_keys(jax.random.fold_in(arg_keys[6], 71), 0)
    values = scatter_about(arg_keys[2], (TOKENS, D), 1.0, 6.0, ((0, 512),))
    out_grad = noise_with(arg_keys[3], (TOKENS, D), 1.0, 24.0, ((0, 512),), (0, 1, 256, 6.0))
    out_weight = scatter_about(arg_keys[4], (D, D), D ** -0.5, 0.21875)
    slide_lengths = jax.vmap(lambda own: ragged(own, SLIDES, GROUP_LEN, GROUP_LEN // 2, 2))(jax.random.split(arg_keys[5], N_DP)).reshape((N_DP, SLIDES)).astype(jnp.int32)
    return {"queries": queries, "keys": keys, "values": values, "out_grad": out_grad, "out_weight": out_weight, "slide_lengths": slide_lengths}


def masked_scores(query, key_rows, ids_q, ids_k):
    scores = jnp.einsum('cqhd,ckhd->cqhk', query.astype(jnp.float32), key_rows.astype(jnp.float32))
    scores = scores * (query.shape[-1] ** -0.5)
    same = ids_q[:, :, None, None] == ids_k[:, None, None, :]
    return jnp.where(same, scores, -jnp.inf)


def attend_forward(query, key_rows, value_rows, ids_q, ids_k):
    scores = masked_scores(query, key_rows, ids_q, ids_k)
    top = jnp.max(scores, -1, keepdims=True)
    expo = jnp.exp(scores - top)
    total = jnp.sum(expo, -1, keepdims=True)
    weights = (expo / total).astype(jnp.bfloat16)
    out = jnp.einsum('cqhk,ckhd->cqhd', weights.astype(jnp.float32), value_rows.astype(jnp.float32))
    return out, top[..., 0] + jnp.log(total[..., 0])


def attend_backward(query, key_rows, value_rows, ids_q, ids_k, dout, lse, delta):
    scale = query.shape[-1] ** -0.5
    scores = masked_scores(query, key_rows, ids_q, ids_k)
    prob = jnp.exp(scores - lse[..., None])
    dvalue = jnp.einsum('cqhk,cqhd->ckhd', prob.astype(jnp.bfloat16).astype(jnp.float32), dout.astype(jnp.float32))
    dprob = jnp.einsum('cqhd,ckhd->cqhk', dout.astype(jnp.float32), value_rows.astype(jnp.float32))
    dscore = (prob * (dprob - delta[..., None]) * scale).astype(jnp.bfloat16).astype(jnp.float32)
    dquery = jnp.einsum('cqhk,ckhd->cqhd', dscore, key_rows.astype(jnp.float32))
    dkey = jnp.einsum('cqhk,cqhd->ckhd', dscore, query.astype(jnp.float32))
    return dquery, dkey, dvalue


def pick(array, spread):
    count, heads, inner = array.shape
    split = array.reshape(count // spread, spread, heads // spread, spread, inner)
    return jnp.stack([split[:, j, :, j, :] for j in range(spread)], 0)


def place(array, spread):
    moved = jnp.transpose(array, (1, 2, 0, 3))
    eye = jnp.eye(spread, dtype=array.dtype)
    full = eye[None, :, None, :, None] * moved[:, None, :, :, :]
    count = moved.shape[0]
    return full.reshape(count * spread, moved.shape[1] * spread, moved.shape[3])


def combine(out_a, lse_a, out_b, lse_b):
    lse = jnp.logaddexp(lse_a, lse_b)
    return jnp.exp(lse_a - lse)[..., None] * out_a + jnp.exp(lse_b - lse)[..., None] * out_b, lse


def group_grads(query, key_rows, value_rows, grad_rows, lengths, weight):
    length = query.shape[0]
    ends = jnp.cumsum(lengths)
    positions = jnp.arange(length, dtype=jnp.int32)
    ids = jnp.sum((positions[:, None] >= ends[None, :]).astype(jnp.int32), -1)
    dout = jnp.dot(grad_rows, weight.T, preferred_element_type=jnp.float32).astype(jnp.bfloat16)
    q3 = query.reshape(length, NHEAD, DH)
    k3 = key_rows.reshape(length, NHEAD, DH)
    v3 = value_rows.reshape(length, NHEAD, DH)
    d3 = dout.reshape(length, NHEAD, DH)
    blocks = length // SEG

    def blocked(array):
        return array.reshape(blocks, SEG, NHEAD, array.shape[-1])

    ids_block = ids.reshape(blocks, SEG)
    out_a, lse_a = attend_forward(blocked(q3), blocked(k3), blocked(v3), ids_block, ids_block)
    out_a = out_a.reshape(length, NHEAD, DH)
    lse_a = lse_a.reshape(length, NHEAD)
    q_sel, k_sel, v_sel, d_sel = pick(q3, DILATION), pick(k3, DILATION), pick(v3, DILATION), pick(d3, DILATION)
    ids_sel = ids.reshape(length // DILATION, DILATION).T
    out_b, lse_b = attend_forward(q_sel, k_sel, v_sel, ids_sel, ids_sel)
    out_c, lse_c = combine(pick(out_a, DILATION), pick(lse_a[..., None], DILATION)[..., 0], out_b, lse_b)
    chosen = place(jnp.ones(lse_c.shape + (1,), jnp.float32), DILATION) > 0.5
    out_full = jnp.where(chosen, place(out_c, DILATION), out_a)
    lse_full = jnp.where(chosen[..., 0], place(lse_c[..., None], DILATION)[..., 0], lse_a)
    attended = out_full.astype(jnp.bfloat16)
    delta = jnp.sum(d3.astype(jnp.float32) * lax.optimization_barrier(attended).astype(jnp.float32), -1)
    dq_a, dk_a, dv_a = attend_backward(blocked(q3), blocked(k3), blocked(v3), ids_block, ids_block, blocked(d3), lse_full.reshape(blocks, SEG, NHEAD), delta.reshape(blocks, SEG, NHEAD))
    delta_sel = pick(delta[..., None], DILATION)[..., 0]
    dq_b, dk_b, dv_b = attend_backward(q_sel, k_sel, v_sel, ids_sel, ids_sel, d_sel, lse_c, delta_sel)
    dq = (dq_a.reshape(length, NHEAD, DH) + place(dq_b, DILATION)).astype(jnp.bfloat16).reshape(length, D)
    dk = (dk_a.reshape(length, NHEAD, DH) + place(dk_b, DILATION)).astype(jnp.bfloat16).reshape(length, D)
    dv = (dv_a.reshape(length, NHEAD, DH) + place(dv_b, DILATION)).astype(jnp.bfloat16).reshape(length, D)
    return dq, dk, dv, attended.reshape(length, D)


def reference(queries, keys, values, out_grad, out_weight, slide_lengths):
    groups = slide_lengths.shape[0]
    shaped = [a.reshape(groups, GROUP_LEN, D) for a in (queries, keys, values, out_grad)]

    def step(total, items):
        query, key_rows, value_rows, grad_rows, lengths = items
        dq, dk, dv, attended = group_grads(query, key_rows, value_rows, grad_rows, lengths, out_weight)
        total = total + jnp.dot(attended.T, grad_rows, preferred_element_type=jnp.float32)
        return total, (dq, dk, dv)

    start = jnp.zeros((D, D), jnp.float32)
    weight_grad, grads = lax.scan(step, start, (shaped[0], shaped[1], shaped[2], shaped[3], slide_lengths))
    dq, dk, dv = grads
    return dq.reshape(TOKENS, D), dk.reshape(TOKENS, D), dv.reshape(TOKENS, D), weight_grad
```

```python
import functools

import jax
import jax.numpy as jnp
from jax import lax
from jax.experimental import pallas as pl
from jax.experimental.pallas import tpu as pltpu
from jax.sharding import PartitionSpec as P

MESH = pl.DeviceIdType.MESH
NHEAD = 16
DH = 48
D = NHEAD * DH
SEG = 256
SPREAD = 8
CLS = SEG // SPREAD
PAIR = 2 * DH
SLIDES = 4
PAD = 16
BIG = 2.0**20
LOG2E = 1.4426950408889634
SCALE = DH**-0.5
F32 = jnp.float32
BF16 = jnp.bfloat16


def iota(shape, dim):
    return lax.broadcasted_iota(jnp.int32, shape, dim)


def mm(a, b):
    return jnp.dot(a, b, preferred_element_type=F32)


def mm_tn(a, b):
    return lax.dot_general(a, b, (((0,), (0,)), ((), ())), preferred_element_type=F32)


def mm_nt(a, b):
    return lax.dot_general(a, b, (((1,), (1,)), ((), ())), preferred_element_type=F32)


def mask_rows(pos, ends):
    row = iota((PAD, pos.shape[1]), 0)
    starts = [0] + ends[:-1]
    hit = jnp.zeros((PAD, pos.shape[1]), F32)
    for i in range(SLIDES):
        inside = jnp.where((pos >= starts[i]) & (pos < ends[i]), 1.0, 0.0)
        hit = jnp.where(row == i, inside, hit)
    off = jnp.where(row < SLIDES, (hit - 1.0) * BIG, 0.0)
    return hit.astype(BF16), off.astype(BF16)


def forward_head(qt, kt, vt, dot, k_mask, q_mask, ones):
    s = mm_tn(jnp.concatenate([kt, k_mask], 0), jnp.concatenate([qt, q_mask], 0))
    top = jnp.max(s, 0, keepdims=True)
    e = jnp.exp2((s - top) * (SCALE * LOG2E)).astype(BF16)
    ov = mm(jnp.concatenate([vt, ones], 0), e)
    total = ov[DH : DH + 1]
    o = ov[:DH] * (1.0 / total)
    top = top * (SCALE * LOG2E)
    lse = top + jnp.log(total) * LOG2E
    delta = jnp.sum(dot.astype(F32) * o, 0, keepdims=True)
    return e, o, top, lse, delta


def backward_head(qt, kt, vt, dot, e, ones, ratio, delta):
    hi = delta.astype(BF16)
    lo = (delta - hi.astype(F32)).astype(BF16)
    row = iota((PAD, delta.shape[1]), 0)
    less = jnp.where(row == 0, -hi.astype(F32), jnp.where(row == 1, -lo.astype(F32), 0.0))
    dp = mm_tn(jnp.concatenate([vt, ones], 0), jnp.concatenate([dot, less.astype(BF16)], 0))
    g = (e.astype(F32) * dp).astype(BF16)
    dv = mm_nt((dot.astype(F32) * ratio).astype(BF16), e)
    ratio = ratio * SCALE
    dk = mm_nt((qt.astype(F32) * ratio).astype(BF16), g)
    dq = mm(kt, g) * ratio
    return dq, dk, dv


def merge(lse_a, delta_a, lse_b, delta_b):
    top = jnp.maximum(lse_a, lse_b)
    lse = top + jnp.log(jnp.exp2(lse_a - top) + jnp.exp2(lse_b - top)) * LOG2E
    w_a, w_b = jnp.exp2(lse_a - lse), jnp.exp2(lse_b - lse)
    return lse, w_a, w_b, w_a * delta_a + w_b * delta_b


def lane_block(rows):
    return iota((rows, 128), 1) // CLS


def shift(x, blocks):
    blocks = blocks % 4
    return x if blocks == 0 else pltpu.roll(x, blocks * CLS, 1)


def kernel(
    q_ref, k_ref, v_ref, g_ref, w_ref, len_ref,
    dq_ref, dk_ref, dv_ref, dw_ref,
    qt, kt, vt, dot, pog, e_all, ot, sta, att, dqt, dkt, dvt,
    qb, kb, vb, db, eb, ob, sb,
    send1, recv1, send2, recv2, send3, recv3, send4, recv4,
    ssem, rsem,
):
    dp = lax.axis_index("dp")
    me = lax.axis_index("seq")

    barrier = pltpu.get_barrier_semaphore()
    for d in range(1, SPREAD):
        pl.semaphore_signal(
            barrier, inc=1, device_id=(dp, lax.rem(me + d, SPREAD)), device_id_type=MESH
        )

    ends = []
    for i in range(SLIDES):
        ends.append(len_ref[0, i] if i == 0 else ends[-1] + len_ref[0, i])

    def exchange(kind, send, recv):
        copies = []
        for d in range(1, SPREAD):
            other = lax.rem(me + d, SPREAD)
            copies.append(
                pltpu.make_async_remote_copy(
                    src_ref=send.at[other],
                    dst_ref=recv.at[me],
                    send_sem=ssem.at[kind, d],
                    recv_sem=rsem.at[kind, d],
                    device_id=(dp, other),
                    device_id_type=MESH,
                )
            )
        return copies

    def arrive(kind, send, recv):
        for d in range(1, SPREAD):
            source = lax.rem(me + SPREAD - d, SPREAD)
            pltpu.make_async_remote_copy(
                src_ref=send.at[source],
                dst_ref=recv.at[source],
                send_sem=ssem.at[kind, d],
                recv_sem=rsem.at[kind, d],
                device_id=(dp, source),
                device_id_type=MESH,
            ).wait_recv()

    to = iota((SEG, SEG), 0)
    at = iota((SEG, SEG), 1)
    perm = jnp.where(at == to % CLS * SPREAD + to // CLS, 1.0, 0.0).astype(BF16)
    for src, dst in ((q_ref, qt), (k_ref, kt), (v_ref, vt)):
        moved = mm(perm, src[...]).T.astype(BF16)
        dst[...] = moved.reshape(NHEAD, DH, SEG)
    pog[...] = mm(perm, g_ref[...]).astype(BF16)
    dot[...] = mm_nt(w_ref[...], pog[...]).astype(BF16).reshape(NHEAD, DH, SEG)

    block = lane_block(PAIR)
    for j in range(SPREAD):
        tile = pl.ds(j // 4 * 128, 128)
        out = jnp.zeros((PAIR, 128), F32)
        for t, src in enumerate((qt, kt, vt, dot)):
            both = jnp.concatenate([src[j, :, tile], src[j + SPREAD, :, tile]], 0)
            out = jnp.where(block == t, shift(both.astype(F32), t - j), out)
        send1[j] = out.astype(BF16)
    recv1[me] = send1[me]

    pl.semaphore_wait(barrier, SPREAD - 1)
    copies1 = exchange(0, send1, recv1)
    for c in copies1:
        c.start()

    lane = iota((1, SEG), 1)
    k_mask, q_mask = mask_rows(me * SEG + lane % CLS * SPREAD + lane // CLS, ends)
    row = iota((PAD, SEG), 0)
    ones = jnp.where(row < 2, 1.0, 0.0).astype(BF16)

    def forward(h, carry):
        e, o, top, lse, delta = forward_head(
            qt[h], kt[h], vt[h], dot[h], k_mask, q_mask, ones
        )
        e_all[h] = e
        ot[h] = o
        sta[h, 0:1] = top
        sta[h, 1:2] = lse
        sta[h, 2:3] = delta
        return carry

    lax.fori_loop(0, NHEAD, forward, 0)

    narrow = lane_block(8)
    for j in range(SPREAD):
        tile = pl.ds(j // 4 * 128, 128)
        rows = jnp.concatenate(
            [sta[j, 1:2, tile], sta[j + SPREAD, 1:2, tile],
             sta[j, 2:3, tile], sta[j + SPREAD, 2:3, tile],
             jnp.zeros((4, 128), F32)], 0)
        send2[j] = shift(rows, -j)
    recv2[me] = send2[me]
    copies2 = exchange(1, send2, recv2)
    for c in copies2:
        c.start()

    arrive(0, send1, recv1)
    for half in range(2):
        tile = pl.ds(half * 128, 128)
        outs = [jnp.zeros((PAIR, 128), F32)] * 4
        for s in range(half * 4, half * 4 + 4):
            got = recv1[s].astype(F32)
            for t in range(4):
                outs[t] = jnp.where(block == s % 4, shift(got, s - t), outs[t])
        for dst, out in zip((qb, kb, vb, db), outs):
            out = out.astype(BF16)
            for u in range(2):
                dst[u, :, tile] = out[u * DH : (u + 1) * DH]
    kb_mask, qb_mask = mask_rows(lane * SPREAD + me, ends)
    for u in range(2):
        e, o, top, lse, delta = forward_head(
            qb[u], kb[u], vb[u], db[u], kb_mask, qb_mask, ones
        )
        eb[u] = e
        ob[u] = o
        sb[u, 0:1] = top
        sb[u, 1:2] = lse
        sb[u, 2:3] = delta

    wide = lane_block(CLS)
    for s in range(SPREAD):
        tile = pl.ds(s // 4 * 128, 128)
        rows = jnp.concatenate(
            [sb[0, 1:2, tile], sb[1, 1:2, tile], sb[0, 2:3, tile], sb[1, 2:3, tile],
             jnp.zeros((4, 128), F32)], 0)
        both = jnp.concatenate([ob[0, :, tile], ob[1, :, tile]], 0)
        out = jnp.zeros((CLS, 128), F32)
        for g in range(3):
            out = jnp.where(wide == g, shift(both[g * CLS : (g + 1) * CLS], g - s), out)
        stat = jnp.concatenate([shift(rows, 3 - s), jnp.zeros((CLS - 8, 128), F32)], 0)
        send3[s] = jnp.where(wide == 3, stat, out)
    recv3[me] = send3[me]
    copies3 = exchange(2, send3, recv3)
    for c in copies3:
        c.start()

    arrive(1, send2, recv2)
    halves = []
    for half in range(2):
        out = jnp.zeros((8, 128), F32)
        for s in range(half * 4, half * 4 + 4):
            out = jnp.where(narrow == s % 4, shift(recv2[s], s), out)
        halves.append(out)
    theirs = jnp.concatenate(halves, 1)
    for u in range(2):
        top = sb[u, 0:1]
        lse, _, _, delta = merge(theirs[u : u + 1], theirs[2 + u : 3 + u], sb[u, 1:2], sb[u, 2:3])
        dq, dk, dv = backward_head(
            qb[u], kb[u], vb[u], db[u], eb[u], ones, jnp.exp2(top - lse), delta
        )
        for s in range(SPREAD):
            tile = slice(s // 4 * 128, s // 4 * 128 + 128)
            out = jnp.zeros((DH, 128), F32)
            for t, x in enumerate((dq, dk, dv)):
                out = jnp.where(lane_block(DH) == t, shift(x[:, tile], t - s), out)
            send4[s, u * DH : (u + 1) * DH] = out.astype(BF16)
    recv4[me] = send4[me]
    copies4 = exchange(3, send4, recv4)
    for c in copies4:
        c.start()

    arrive(2, send3, recv3)
    tall = iota((NHEAD, 128), 0)
    spot = lane_block(NHEAD)
    lse_b, delta_b = [], []
    for half in range(2):
        lb = jnp.full((NHEAD, 128), -1e30, F32)
        dbl = jnp.zeros((NHEAD, 128), F32)
        for j in range(half * 4, half * 4 + 4):
            x = shift(recv3[j, 0:8], j - 3)
            for u in range(2):
                here = (tall == j + SPREAD * u) & (spot == j % 4)
                lb = jnp.where(here, x[u : u + 1], lb)
                dbl = jnp.where(here, x[2 + u : 3 + u], dbl)
        lse_b.append(lb)
        delta_b.append(dbl)
    lse_b, delta_b = jnp.concatenate(lse_b, 1), jnp.concatenate(delta_b, 1)
    lse, w_a, w_b, delta = merge(sta[:, 1, :], sta[:, 2, :], lse_b, delta_b)
    sta[:, 2, :] = delta
    sta[:, 3, :] = jnp.exp2(sta[:, 0, :] - lse)
    for j in range(SPREAD):
        got = recv3[j]
        other = jnp.concatenate([shift(got, j - g) for g in range(3)], 0)
        for u in range(2):
            h = j + SPREAD * u
            for half in range(2):
                tile = slice(half * 128, half * 128 + 128)
                x = ot[h, :, tile] * w_a[h : h + 1, tile]
                if half == j // 4:
                    part = other[u * DH : (u + 1) * DH] * w_b[h : h + 1, tile]
                    x = x + jnp.where(lane_block(DH) == j % 4, part, 0.0)
                att[h * DH : (h + 1) * DH, tile] = x.astype(BF16)
    dw_ref[...] = mm(att[...], pog[...])

    def backward(h, carry):
        dq, dk, dv = backward_head(
            qt[h], kt[h], vt[h], dot[h], e_all[h], ones, sta[h, 3:4], sta[h, 2:3]
        )
        dqt[h] = dq
        dkt[h] = dk
        dvt[h] = dv
        return carry

    lax.fori_loop(0, NHEAD, backward, 0)

    arrive(3, send4, recv4)
    for j in range(SPREAD):
        tile = pl.ds(j // 4 * 128, 128)
        got = recv4[j].astype(F32)
        for t, dst in enumerate((dqt, dkt, dvt)):
            part = jnp.where(block == j % 4, shift(got, j - t), 0.0)
            for u in range(2):
                h = j + SPREAD * u
                dst[h, :, tile] = dst[h, :, tile] + part[u * DH : (u + 1) * DH]
    back = jnp.where(to == at % CLS * SPREAD + at // CLS, 1.0, 0.0).astype(BF16)
    for src, dst in ((dqt, dq_ref), (dkt, dk_ref), (dvt, dv_ref)):
        dst[...] = mm_nt(back, src[...].reshape(D, SEG).astype(BF16)).astype(BF16)

    for c in copies1 + copies2 + copies3 + copies4:
        c.wait_send()


def on_device(queries, keys, values, out_grad, out_weight, slide_lengths):
    vmem = pl.BlockSpec(memory_space=pltpu.VMEM)
    heads = lambda n, dtype: pltpu.VMEM((n, DH, SEG), dtype)
    dq, dk, dv, partial = pl.pallas_call(
        kernel,
        out_shape=(
            jax.ShapeDtypeStruct((SEG, D), BF16),
            jax.ShapeDtypeStruct((SEG, D), BF16),
            jax.ShapeDtypeStruct((SEG, D), BF16),
            jax.ShapeDtypeStruct((D, D), F32),
        ),
        in_specs=[vmem] * 5 + [pl.BlockSpec(memory_space=pltpu.SMEM)],
        out_specs=(vmem,) * 4,
        scratch_shapes=[
            heads(NHEAD, BF16), heads(NHEAD, BF16), heads(NHEAD, BF16), heads(NHEAD, BF16),
            pltpu.VMEM((SEG, D), BF16),
            pltpu.VMEM((NHEAD, SEG, SEG), BF16),
            heads(NHEAD, F32),
            pltpu.VMEM((NHEAD, 8, SEG), F32),
            pltpu.VMEM((D, SEG), BF16),
            heads(NHEAD, F32), heads(NHEAD, F32), heads(NHEAD, F32),
            heads(2, BF16), heads(2, BF16), heads(2, BF16), heads(2, BF16),
            pltpu.VMEM((2, SEG, SEG), BF16),
            heads(2, F32),
            pltpu.VMEM((2, 8, SEG), F32),
            pltpu.VMEM((SPREAD, PAIR, 128), BF16), pltpu.VMEM((SPREAD, PAIR, 128), BF16),
            pltpu.VMEM((SPREAD, 8, 128), F32), pltpu.VMEM((SPREAD, 8, 128), F32),
            pltpu.VMEM((SPREAD, CLS, 128), F32), pltpu.VMEM((SPREAD, CLS, 128), F32),
            pltpu.VMEM((SPREAD, PAIR, 128), BF16), pltpu.VMEM((SPREAD, PAIR, 128), BF16),
            pltpu.SemaphoreType.DMA((4, SPREAD)),
            pltpu.SemaphoreType.DMA((4, SPREAD)),
        ],
        compiler_params=pltpu.CompilerParams(
            collective_id=0, has_side_effects=True, vmem_limit_bytes=48 * 1024 * 1024
        ),
    )(queries, keys, values, out_grad, out_weight, slide_lengths)
    rows_mine = lax.psum_scatter(partial, "dp", scatter_dimension=0, tiled=True)
    weight_grad = lax.psum_scatter(rows_mine, "seq", scatter_dimension=1, tiled=True)
    return dq, dk, dv, weight_grad


def solution(mesh):
    placed = (
        P(("dp", "seq"), None),
        P(("dp", "seq"), None),
        P(("dp", "seq"), None),
        P(("dp", "seq"), None),
        P(),
        P("dp", None),
    )
    return jax.shard_map(
        on_device,
        mesh=mesh,
        in_specs=placed,
        out_specs=(
            P(("dp", "seq"), None),
            P(("dp", "seq"), None),
            P(("dp", "seq"), None),
            P("dp", "seq"),
        ),
        check_vma=False,
    )
```

```python
import functools

import jax
import jax.numpy as jnp
from jax import lax
from jax.experimental import pallas as pl
from jax.experimental.pallas import tpu as pltpu
from jax.sharding import PartitionSpec as P

MESH = pl.DeviceIdType.MESH
NHEAD = 16
DH = 48
D = NHEAD * DH
SEG = 256
SPREAD = 8
CLS = SEG // SPREAD
PAIR = 2 * DH
SLIDES = 4
NX = 4
NY = 4
NZ = 16
COLS = D // SPREAD
COLH = D // 2
PAD = 16
BIG = 2.0**20
LOG2E = 1.4426950408889634
SCALE = DH**-0.5
F32 = jnp.float32
BF16 = jnp.bfloat16


def iota(shape, dim):
    return lax.broadcasted_iota(jnp.int32, shape, dim)


def mm(a, b):
    return jnp.dot(a, b, preferred_element_type=F32)


def mm_tn(a, b):
    return lax.dot_general(a, b, (((0,), (0,)), ((), ())), preferred_element_type=F32)


def mm_nt(a, b):
    return lax.dot_general(a, b, (((1,), (1,)), ((), ())), preferred_element_type=F32)


def mask_rows(pos, ends):
    row = iota((PAD, pos.shape[1]), 0)
    starts = [0] + ends[:-1]
    hit = jnp.zeros((PAD, pos.shape[1]), F32)
    for i in range(SLIDES):
        inside = jnp.where((pos >= starts[i]) & (pos < ends[i]), 1.0, 0.0)
        hit = jnp.where(row == i, inside, hit)
    off = jnp.where(row < SLIDES, (hit - 1.0) * BIG, 0.0)
    return hit.astype(BF16), off.astype(BF16)


def forward_head(qt, kt, vt, dot, k_mask, q_mask, ones):
    s = mm_tn(jnp.concatenate([kt, k_mask], 0), jnp.concatenate([qt, q_mask], 0))
    top = jnp.max(s, 0, keepdims=True)
    e = jnp.exp2((s - top) * (SCALE * LOG2E)).astype(BF16)
    ov = mm(jnp.concatenate([vt, ones], 0), e)
    total = ov[DH : DH + 1]
    o = ov[:DH] * (1.0 / total)
    top = top * (SCALE * LOG2E)
    lse = top + jnp.log(total) * LOG2E
    delta = jnp.sum(dot.astype(F32) * o, 0, keepdims=True)
    return e, o, top, lse, delta


def backward_head(qt, kt, vt, dot, e, ones, ratio, delta):
    hi = delta.astype(BF16)
    lo = (delta - hi.astype(F32)).astype(BF16)
    row = iota((PAD, delta.shape[1]), 0)
    less = jnp.where(row == 0, -hi.astype(F32), jnp.where(row == 1, -lo.astype(F32), 0.0))
    dp = mm_tn(jnp.concatenate([vt, ones], 0), jnp.concatenate([dot, less.astype(BF16)], 0))
    g = (e.astype(F32) * dp).astype(BF16)
    dv = mm_nt((dot.astype(F32) * ratio).astype(BF16), e)
    ratio = ratio * SCALE
    dk = mm_nt((qt.astype(F32) * ratio).astype(BF16), g)
    dq = mm(kt, g) * ratio
    return dq, dk, dv


def merge(lse_a, delta_a, lse_b, delta_b):
    top = jnp.maximum(lse_a, lse_b)
    lse = top + jnp.log(jnp.exp2(lse_a - top) + jnp.exp2(lse_b - top)) * LOG2E
    w_a, w_b = jnp.exp2(lse_a - lse), jnp.exp2(lse_b - lse)
    return lse, w_a, w_b, w_a * delta_a + w_b * delta_b


def lane_block(rows):
    return iota((rows, 128), 1) // CLS


def pick_rows(count, step, width, padded):
    r = iota((count * padded, width), 0)
    at = iota((count * padded, width), 1)
    inside = (r % padded < step) & (at == r // padded * step + r % padded)
    return jnp.where(inside, 1.0, 0.0).astype(BF16)


def up(n, to):
    return (n + to - 1) // to * to


def shift(x, blocks):
    blocks = blocks % 4
    return x if blocks == 0 else pltpu.roll(x, blocks * CLS, 1)


def kernel(
    q_in, k_in, v_in, g_in, w_in, len_ref,
    dq_ref, dk_ref, dv_ref, dw_ref,
    q_ref, k_ref, v_ref, g_ref, w_ref, isem,
    qt, kt, vt, dot, pog, e_all, ot, sta, att, dqt, dkt, dvt,
    qb, kb, vb, db, eb, ob, sb,
    send1, recv1, send2, recv2, send3, recv3, send4, recv4,
    ssem, rsem,
    ogt, c_send, c_recv, a1_send, a1_recv, a2_send, a2_recv, b1_send, b1_recv, b2_send, b2_recv,
    z_send, z_recv, c_sem, a1_sem, a2_sem, b1_sem, b2_sem, z_sem,
):
    dp = lax.axis_index("dp")
    me = lax.axis_index("seq")
    my, mz, mx, mc = dp // NZ, dp % NZ, me // 2, me % 2
    half_rows = D // NY // 2
    wide_rows = up(half_rows, 128)
    z_rows = D // (NY * NZ)
    z_pad = up(z_rows, 16)

    loads = []
    for i, (src, dst) in enumerate(
        ((q_in, q_ref), (k_in, k_ref), (v_in, v_ref), (g_in, g_ref), (w_in, w_ref))
    ):
        loads.append(pltpu.make_async_copy(src, dst, isem.at[i]))
        loads[-1].start()

    barrier = pltpu.get_barrier_semaphore()
    for d in range(1, SPREAD):
        pl.semaphore_signal(
            barrier, inc=1, device_id=(dp, lax.rem(me + d, SPREAD)), device_id_type=MESH
        )
    for d in range(1, NY):
        pl.semaphore_signal(
            barrier, inc=1, device_id=(lax.rem(my + d, NY) * NZ + mz, me), device_id_type=MESH
        )
    for d in range(1, NZ):
        pl.semaphore_signal(
            barrier, inc=1, device_id=(my * NZ + lax.rem(mz + d, NZ), me), device_id_type=MESH
        )

    ends = []
    for i in range(SLIDES):
        ends.append(len_ref[0, i] if i == 0 else ends[-1] + len_ref[0, i])

    def exchange(kind, send, recv):
        copies = []
        for d in range(1, SPREAD):
            other = lax.rem(me + d, SPREAD)
            copies.append(
                pltpu.make_async_remote_copy(
                    src_ref=send.at[other],
                    dst_ref=recv.at[me],
                    send_sem=ssem.at[kind, d],
                    recv_sem=rsem.at[kind, d],
                    device_id=(dp, other),
                    device_id_type=MESH,
                )
            )
        return copies

    def arrive(kind, send, recv):
        for d in range(1, SPREAD):
            source = lax.rem(me + SPREAD - d, SPREAD)
            pltpu.make_async_remote_copy(
                src_ref=send.at[source],
                dst_ref=recv.at[source],
                send_sem=ssem.at[kind, d],
                recv_sem=rsem.at[kind, d],
                device_id=(dp, source),
                device_id_type=MESH,
            ).wait_recv()

    def along(size, place, device, send, recv, sem):
        def copy(d, slot, other):
            return pltpu.make_async_remote_copy(
                src_ref=send.at[other],
                dst_ref=recv.at[slot],
                send_sem=sem.at[0, d],
                recv_sem=sem.at[1, d],
                device_id=device(other),
                device_id_type=MESH,
            )

        def start():
            recv[place] = send[place]
            for d in range(1, size):
                copy(d, place, lax.rem(place + d, size)).start()

        def finish():
            for d in range(1, size):
                source = lax.rem(place + size - d, size)
                copy(d, source, source).wait_recv()

        def sent():
            for d in range(1, size):
                copy(d, place, lax.rem(place + d, size)).wait_send()

        return start, finish, sent

    def across(send, recv, sem):
        def copy(b, slot, other):
            return pltpu.make_async_remote_copy(
                src_ref=send.at[b],
                dst_ref=recv.at[slot],
                send_sem=sem.at[0, b],
                recv_sem=sem.at[1, slot],
                device_id=(dp, other),
                device_id_type=MESH,
            )

        def start():
            for b in range(NX):
                other = 4 * mc + b

                @pl.when(other != me)
                def _():
                    copy(b, mx, other).start()

                @pl.when(other == me)
                def _():
                    recv[mx] = send[b]

        def finish():
            for x in range(NX):
                source = 2 * x + me // 4

                @pl.when(source != me)
                def _():
                    copy(0, x, source).wait_recv()

        def sent():
            for b in range(NX):
                other = 4 * mc + b

                @pl.when(other != me)
                def _():
                    copy(b, mx, other).wait_send()

        return start, finish, sent

    def total(recv, count):
        out = recv[0].astype(F32)
        for i in range(1, count):
            out = out + recv[i].astype(F32)
        return out

    to = iota((SEG, SEG), 0)
    at = iota((SEG, SEG), 1)
    perm = jnp.where(at == to % CLS * SPREAD + to // CLS, 1.0, 0.0).astype(BF16)
    for i, (src, dst) in enumerate(((q_ref, qt), (k_ref, kt), (v_ref, vt))):
        loads[i].wait()
        moved = mm(perm, src[...]).T.astype(BF16)
        dst[...] = moved.reshape(NHEAD, DH, SEG)
    loads[3].wait()
    loads[4].wait()
    pog[...] = mm(perm, g_ref[...]).astype(BF16)
    dot[...] = mm_nt(w_ref[...], pog[...]).astype(BF16).reshape(NHEAD, DH, SEG)

    block = lane_block(PAIR)
    for j in range(SPREAD):
        tile = pl.ds(j // 4 * 128, 128)
        out = jnp.zeros((PAIR, 128), F32)
        for t, src in enumerate((qt, kt, vt, dot)):
            both = jnp.concatenate([src[j, :, tile], src[j + SPREAD, :, tile]], 0)
            out = jnp.where(block == t, shift(both.astype(F32), t - j), out)
        send1[j] = out.astype(BF16)
    recv1[me] = send1[me]

    pl.semaphore_wait(barrier, SPREAD - 1 + NY - 1 + NZ - 1)
    copies1 = exchange(0, send1, recv1)
    for c in copies1:
        c.start()

    lane = iota((1, SEG), 1)
    k_mask, q_mask = mask_rows(me * SEG + lane % CLS * SPREAD + lane // CLS, ends)
    row = iota((PAD, SEG), 0)
    ones = jnp.where(row < 2, 1.0, 0.0).astype(BF16)

    def forward(h, carry):
        e, o, top, lse, delta = forward_head(
            qt[h], kt[h], vt[h], dot[h], k_mask, q_mask, ones
        )
        e_all[h] = e
        ot[h] = o
        sta[h, 0:1] = top
        sta[h, 1:2] = lse
        sta[h, 2:3] = delta
        return carry

    lax.fori_loop(0, NHEAD, forward, 0)
    ogt[...] = pog[...].T

    narrow = lane_block(8)
    for j in range(SPREAD):
        tile = pl.ds(j // 4 * 128, 128)
        rows = jnp.concatenate(
            [sta[j, 1:2, tile], sta[j + SPREAD, 1:2, tile],
             sta[j, 2:3, tile], sta[j + SPREAD, 2:3, tile],
             jnp.zeros((4, 128), F32)], 0)
        send2[j] = shift(rows, -j)
    recv2[me] = send2[me]
    copies2 = exchange(1, send2, recv2)
    for c in copies2:
        c.start()

    arrive(0, send1, recv1)
    for half in range(2):
        tile = pl.ds(half * 128, 128)
        outs = [jnp.zeros((PAIR, 128), F32)] * 4
        for s in range(half * 4, half * 4 + 4):
            got = recv1[s].astype(F32)
            for t in range(4):
                outs[t] = jnp.where(block == s % 4, shift(got, s - t), outs[t])
        for dst, out in zip((qb, kb, vb, db), outs):
            out = out.astype(BF16)
            for u in range(2):
                dst[u, :, tile] = out[u * DH : (u + 1) * DH]
    kb_mask, qb_mask = mask_rows(lane * SPREAD + me, ends)
    for u in range(2):
        e, o, top, lse, delta = forward_head(
            qb[u], kb[u], vb[u], db[u], kb_mask, qb_mask, ones
        )
        eb[u] = e
        ob[u] = o
        sb[u, 0:1] = top
        sb[u, 1:2] = lse
        sb[u, 2:3] = delta

    wide = lane_block(CLS)
    for s in range(SPREAD):
        tile = pl.ds(s // 4 * 128, 128)
        rows = jnp.concatenate(
            [sb[0, 1:2, tile], sb[1, 1:2, tile], sb[0, 2:3, tile], sb[1, 2:3, tile],
             jnp.zeros((4, 128), F32)], 0)
        both = jnp.concatenate([ob[0, :, tile], ob[1, :, tile]], 0)
        out = jnp.zeros((CLS, 128), F32)
        for g in range(3):
            out = jnp.where(wide == g, shift(both[g * CLS : (g + 1) * CLS], g - s), out)
        stat = jnp.concatenate([shift(rows, 3 - s), jnp.zeros((CLS - 8, 128), F32)], 0)
        send3[s] = jnp.where(wide == 3, stat, out)
    recv3[me] = send3[me]
    copies3 = exchange(2, send3, recv3)
    for c in copies3:
        c.start()

    arrive(2, send3, recv3)
    tall = iota((NHEAD, 128), 0)
    spot = lane_block(NHEAD)
    lse_b, delta_b = [], []
    for half in range(2):
        lb = jnp.full((NHEAD, 128), -1e30, F32)
        dbl = jnp.zeros((NHEAD, 128), F32)
        for j in range(half * 4, half * 4 + 4):
            x = shift(recv3[j, 0:8], j - 3)
            for u in range(2):
                here = (tall == j + SPREAD * u) & (spot == j % 4)
                lb = jnp.where(here, x[u : u + 1], lb)
                dbl = jnp.where(here, x[2 + u : 3 + u], dbl)
        lse_b.append(lb)
        delta_b.append(dbl)
    lse_b, delta_b = jnp.concatenate(lse_b, 1), jnp.concatenate(delta_b, 1)
    lse, w_a, w_b, delta = merge(sta[:, 1, :], sta[:, 2, :], lse_b, delta_b)
    sta[:, 2, :] = delta
    sta[:, 3, :] = jnp.exp2(sta[:, 0, :] - lse)
    for j in range(SPREAD):
        got = recv3[j]
        other = jnp.concatenate([shift(got, j - g) for g in range(3)], 0)
        for u in range(2):
            h = j + SPREAD * u
            for half in range(2):
                tile = slice(half * 128, half * 128 + 128)
                x = ot[h, :, tile] * w_a[h : h + 1, tile]
                if half == j // 4:
                    part = other[u * DH : (u + 1) * DH] * w_b[h : h + 1, tile]
                    x = x + jnp.where(lane_block(DH) == j % 4, part, 0.0)
                att[h * DH : (h + 1) * DH, tile] = x.astype(BF16)
    def part(which, side):
        rows = [
            att[y * 2 * half_rows + which * half_rows : y * 2 * half_rows + (which + 1) * half_rows]
            for y in range(NY)
        ]
        rows = jnp.concatenate(rows, 0)
        if which == 0:
            return mm(rows, pog[:, pl.ds(pl.multiple_of(side * COLH, 128), COLH)])
        return mm_nt(ogt[pl.ds(pl.multiple_of(side * COLH, 128), COLH)], rows)

    sibling = [
        pltpu.make_async_remote_copy(
            src_ref=c_send.at[i],
            dst_ref=c_recv.at[i],
            send_sem=c_sem.at[0, i],
            recv_sem=c_sem.at[1, i],
            device_id=(dp, 2 * mx + 1 - mc),
            device_id_type=MESH,
        )
        for i in range(2)
    ]
    for i in range(2):
        c_send[i] = part(i, 1 - mc).astype(BF16)
        sibling[i].start()
    a1 = along(NY, my, lambda y: (y * NZ + mz, me), a1_send, a1_recv, a1_sem)
    a2 = across(a2_send, a2_recv, a2_sem)
    b1 = across(b1_send, b1_recv, b1_sem)
    b2 = along(NY, my, lambda y: (y * NZ + mz, me), b2_send, b2_recv, b2_sem)
    zz = along(NZ, mz, lambda z: (my * NZ + z, me), z_send, z_recv, z_sem)

    def step_a():
        for i, (send, count, step) in enumerate(((a1_send, NY, a1), (a2_send, NX, a2))):
            own = part(i, mc)
            sibling[i].wait_recv()
            own = (own + c_recv[i].astype(F32)).astype(BF16)
            for n in range(count):
                send[n] = own[n * COLH // count : (n + 1) * COLH // count]
            step[0]()

    def step_b():
        a1[1]()
        x = total(a1_recv, NY).astype(BF16)
        x = mm_nt(x, pick_rows(NX, COLS, COLH, 128)).astype(BF16)
        for b in range(NX):
            b1_send[b] = x[:, b * 128 : (b + 1) * 128]
        b1[0]()
        a2[1]()
        x = total(a2_recv, NX).astype(BF16)
        x = mm_nt(x, pick_rows(NY, half_rows, COLH, wide_rows)).astype(BF16)
        for y in range(NY):
            b2_send[y] = x[:, y * wide_rows : (y + 1) * wide_rows]
        b2[0]()

    def step_z():
        pick = pick_rows(NZ // 2, z_rows, wide_rows, z_pad)
        b1[1]()
        x = total(b1_recv, NX)
        x = jnp.concatenate([x, jnp.zeros((wide_rows - half_rows, 128), F32)], 0)
        x = mm(pick, x.astype(BF16)).astype(BF16)
        for z in range(NZ // 2):
            z_send[z] = x[z * z_pad : (z + 1) * z_pad]
        b2[1]()
        x = total(b2_recv, NY)
        x = jnp.concatenate([x, jnp.zeros((128 - COLS, wide_rows), F32)], 0)
        x = mm_nt(pick, x.astype(BF16)).astype(BF16)
        for z in range(NZ // 2):
            z_send[NZ // 2 + z] = x[z * z_pad : (z + 1) * z_pad]
        zz[0]()

    def finish():
        zz[1]()
        dw_ref[...] = total(z_recv, NZ)[:z_rows, :COLS]

    arrive(1, send2, recv2)
    halves = []
    for half in range(2):
        out = jnp.zeros((8, 128), F32)
        for s in range(half * 4, half * 4 + 4):
            out = jnp.where(narrow == s % 4, shift(recv2[s], s), out)
        halves.append(out)
    theirs = jnp.concatenate(halves, 1)
    for u in range(2):
        top = sb[u, 0:1]
        lse, _, _, delta = merge(theirs[u : u + 1], theirs[2 + u : 3 + u], sb[u, 1:2], sb[u, 2:3])
        dq, dk, dv = backward_head(
            qb[u], kb[u], vb[u], db[u], eb[u], ones, jnp.exp2(top - lse), delta
        )
        for s in range(SPREAD):
            tile = slice(s // 4 * 128, s // 4 * 128 + 128)
            out = jnp.zeros((DH, 128), F32)
            for t, x in enumerate((dq, dk, dv)):
                out = jnp.where(lane_block(DH) == t, shift(x[:, tile], t - s), out)
            send4[s, u * DH : (u + 1) * DH] = out.astype(BF16)
    recv4[me] = send4[me]
    copies4 = exchange(3, send4, recv4)
    for c in copies4:
        c.start()

    def backward(h, carry):
        dq, dk, dv = backward_head(
            qt[h], kt[h], vt[h], dot[h], e_all[h], ones, sta[h, 3:4], sta[h, 2:3]
        )
        dqt[h] = dq
        dkt[h] = dk
        dvt[h] = dv
        return carry

    step_a()
    lax.fori_loop(0, NHEAD // 2, backward, 0)
    step_b()
    lax.fori_loop(NHEAD // 2, NHEAD, backward, 0)
    step_z()

    arrive(3, send4, recv4)
    for j in range(SPREAD):
        tile = pl.ds(j // 4 * 128, 128)
        got = recv4[j].astype(F32)
        for t, dst in enumerate((dqt, dkt, dvt)):
            part = jnp.where(block == j % 4, shift(got, j - t), 0.0)
            for u in range(2):
                h = j + SPREAD * u
                dst[h, :, tile] = dst[h, :, tile] + part[u * DH : (u + 1) * DH]
    back = jnp.where(to == at % CLS * SPREAD + at // CLS, 1.0, 0.0).astype(BF16)
    for src, dst in ((dqt, dq_ref), (dkt, dk_ref), (dvt, dv_ref)):
        dst[...] = mm_nt(back, src[...].reshape(D, SEG).astype(BF16)).astype(BF16)

    finish()
    for c in copies1 + copies2 + copies3 + copies4 + sibling:
        c.wait_send()
    for step in (a1, a2, b1, b2, zz):
        step[2]()


def on_device(queries, keys, values, out_grad, out_weight, slide_lengths):
    vmem = pl.BlockSpec(memory_space=pltpu.VMEM)
    heads = lambda n, dtype: pltpu.VMEM((n, DH, SEG), dtype)
    half_rows = D // NY // 2
    wide_rows = up(half_rows, 128)
    z_rows = D // (NY * NZ)
    z_pad = up(z_rows, 16)
    return pl.pallas_call(
        kernel,
        out_shape=(
            jax.ShapeDtypeStruct((SEG, D), BF16),
            jax.ShapeDtypeStruct((SEG, D), BF16),
            jax.ShapeDtypeStruct((SEG, D), BF16),
            jax.ShapeDtypeStruct((z_rows, COLS), F32),
        ),
        in_specs=[pl.BlockSpec(memory_space=pl.ANY)] * 5 + [pl.BlockSpec(memory_space=pltpu.SMEM)],
        out_specs=(vmem,) * 4,
        scratch_shapes=[
            pltpu.VMEM((SEG, D), BF16), pltpu.VMEM((SEG, D), BF16), pltpu.VMEM((SEG, D), BF16),
            pltpu.VMEM((SEG, D), BF16), pltpu.VMEM((D, D), BF16),
            pltpu.SemaphoreType.DMA((5,)),
            heads(NHEAD, BF16), heads(NHEAD, BF16), heads(NHEAD, BF16), heads(NHEAD, BF16),
            pltpu.VMEM((SEG, D), BF16),
            pltpu.VMEM((NHEAD, SEG, SEG), BF16),
            heads(NHEAD, F32),
            pltpu.VMEM((NHEAD, 8, SEG), F32),
            pltpu.VMEM((D, SEG), BF16),
            heads(NHEAD, F32), heads(NHEAD, F32), heads(NHEAD, F32),
            heads(2, BF16), heads(2, BF16), heads(2, BF16), heads(2, BF16),
            pltpu.VMEM((2, SEG, SEG), BF16),
            heads(2, F32),
            pltpu.VMEM((2, 8, SEG), F32),
            pltpu.VMEM((SPREAD, PAIR, 128), BF16), pltpu.VMEM((SPREAD, PAIR, 128), BF16),
            pltpu.VMEM((SPREAD, 8, 128), F32), pltpu.VMEM((SPREAD, 8, 128), F32),
            pltpu.VMEM((SPREAD, CLS, 128), F32), pltpu.VMEM((SPREAD, CLS, 128), F32),
            pltpu.VMEM((SPREAD, PAIR, 128), BF16), pltpu.VMEM((SPREAD, PAIR, 128), BF16),
            pltpu.SemaphoreType.DMA((4, SPREAD)),
            pltpu.SemaphoreType.DMA((4, SPREAD)),
            pltpu.VMEM((D, SEG), BF16),
            pltpu.VMEM((2, COLH, COLH), BF16), pltpu.VMEM((2, COLH, COLH), BF16),
            pltpu.VMEM((NY, half_rows, COLH), BF16), pltpu.VMEM((NY, half_rows, COLH), BF16),
            pltpu.VMEM((NX, COLS, COLH), BF16), pltpu.VMEM((NX, COLS, COLH), BF16),
            pltpu.VMEM((NX, half_rows, 128), BF16), pltpu.VMEM((NX, half_rows, 128), BF16),
            pltpu.VMEM((NY, COLS, wide_rows), BF16), pltpu.VMEM((NY, COLS, wide_rows), BF16),
            pltpu.VMEM((NZ, z_pad, 128), BF16), pltpu.VMEM((NZ, z_pad, 128), BF16),
            pltpu.SemaphoreType.DMA((2, 2)),
            pltpu.SemaphoreType.DMA((2, NY)), pltpu.SemaphoreType.DMA((2, NX)),
            pltpu.SemaphoreType.DMA((2, NX)), pltpu.SemaphoreType.DMA((2, NY)),
            pltpu.SemaphoreType.DMA((2, NZ)),
        ],
        compiler_params=pltpu.CompilerParams(
            collective_id=0, has_side_effects=True, vmem_limit_bytes=48 * 1024 * 1024
        ),
    )(queries, keys, values, out_grad, out_weight, slide_lengths)


def solution(mesh):
    placed = (
        P(("dp", "seq"), None),
        P(("dp", "seq"), None),
        P(("dp", "seq"), None),
        P(("dp", "seq"), None),
        P(),
        P("dp", None),
    )
    return jax.shard_map(
        on_device,
        mesh=mesh,
        in_specs=placed,
        out_specs=(
            P(("dp", "seq"), None),
            P(("dp", "seq"), None),
            P(("dp", "seq"), None),
            P("dp", "seq"),
        ),
        check_vma=False,
    )
```

```python
import functools

import jax
import jax.numpy as jnp
from jax import lax
from jax.experimental import pallas as pl
from jax.experimental.pallas import tpu as pltpu
from jax.sharding import PartitionSpec as P

MESH = pl.DeviceIdType.MESH
NHEAD = 16
DH = 48
D = NHEAD * DH
SEG = 256
SPREAD = 8
CLS = SEG // SPREAD
PAIR = 2 * DH
DENSE = PAIR // 4
PACK1 = 32
PACK3 = 80
SLIDES = 4
NX = 4
UF = 8
UB = 8
NY = 4
NZ = 16
COLS = D // SPREAD
COLH = D // 2
PAD = 16
BIG = 2.0**20
VMEM_LIMIT = 60 * 1024 * 1024
LOG2E = 1.4426950408889634
SCALE = DH**-0.5
F32 = jnp.float32
BF16 = jnp.bfloat16


def iota(shape, dim):
    return lax.broadcasted_iota(jnp.int32, shape, dim)


def mm(a, b):
    return jnp.dot(a, b, preferred_element_type=F32)


def mm_tn(a, b):
    return lax.dot_general(a, b, (((0,), (0,)), ((), ())), preferred_element_type=F32)


def mm_nt(a, b):
    return lax.dot_general(a, b, (((1,), (1,)), ((), ())), preferred_element_type=F32)


def mask_rows(pos, ends):
    row = iota((PAD, pos.shape[1]), 0)
    starts = [0] + ends[:-1]
    hit = jnp.zeros((PAD, pos.shape[1]), F32)
    for i in range(SLIDES):
        inside = jnp.where((pos >= starts[i]) & (pos < ends[i]), 1.0, 0.0)
        hit = jnp.where(row == i, inside, hit)
    off = jnp.where(row < SLIDES, (hit - 1.0) * BIG, 0.0)
    return hit.astype(BF16), off.astype(BF16)


def scores(qt, kt, k_mask, q_mask):
    return mm_tn(jnp.concatenate([kt, k_mask], 0), jnp.concatenate([qt, q_mask], 0))


def weigh(s, top, vt, ones):
    top = top * (SCALE * LOG2E)
    e = jnp.exp2(s * (SCALE * LOG2E) - top).astype(BF16)
    ov = mm(jnp.concatenate([vt, ones], 0), e)
    total = ov[DH : DH + 1]
    return e, ov[:DH] * (1.0 / total), top, top + jnp.log(total) * LOG2E


def forward_head(qt, kt, vt, k_mask, q_mask, ones):
    s = scores(qt, kt, k_mask, q_mask)
    return weigh(s, jnp.max(s, 0, keepdims=True), vt, ones)


def backward_head(qt, kt, vt, dot, e, ones, ratio, delta):
    hi = delta.astype(BF16)
    lo = (delta - hi.astype(F32)).astype(BF16)
    row = iota((PAD, delta.shape[1]), 0)
    less = jnp.where(row == 0, -hi.astype(F32), jnp.where(row == 1, -lo.astype(F32), 0.0))
    dp = mm_tn(jnp.concatenate([vt, ones], 0), jnp.concatenate([dot, less.astype(BF16)], 0))
    g = (e.astype(F32) * dp).astype(BF16)
    dv = mm_nt((dot.astype(F32) * ratio).astype(BF16), e)
    ratio = ratio * SCALE
    dk = mm_nt((qt.astype(F32) * ratio).astype(BF16), g)
    dq = mm(kt, g) * ratio
    return dq, dk, dv


def merge(lse_a, delta_a, lse_b, delta_b):
    top = jnp.maximum(lse_a, lse_b)
    lse = top + jnp.log(jnp.exp2(lse_a - top) + jnp.exp2(lse_b - top)) * LOG2E
    w_a, w_b = jnp.exp2(lse_a - lse), jnp.exp2(lse_b - lse)
    return lse, w_a, w_b, w_a * delta_a + w_b * delta_b


def lane_block(rows):
    return iota((rows, 128), 1) // CLS


def pick_rows(count, step, width, padded):
    r = iota((count * padded, width), 0)
    at = iota((count * padded, width), 1)
    inside = (r % padded < step) & (at == r // padded * step + r % padded)
    return jnp.where(inside, 1.0, 0.0).astype(BF16)


def up(n, to):
    return (n + to - 1) // to * to


def shift(x, blocks):
    blocks = blocks % 4
    return x if blocks == 0 else pltpu.roll(x, blocks * CLS, 1)


def pack(parts, j, rows):
    out = []
    block = lane_block(DENSE)
    for x in parts:
        dense = jnp.zeros((DENSE, 128), F32)
        for b in range(4):
            dense = jnp.where(block == b, shift(x[b * DENSE : (b + 1) * DENSE], b - j), dense)
        out.append(dense)
    out.append(jnp.zeros((rows - len(parts) * DENSE, 128), F32))
    return jnp.concatenate(out, 0)


def unpack(x, t, j):
    x = x[t * DENSE : (t + 1) * DENSE]
    return jnp.concatenate([shift(x, j - b) for b in range(4)], 0)


def kernel(
    q_in, k_in, v_in, g_in, w_in, len_ref,
    grads_ref, dw_ref,
    q_ref, k_ref, v_ref, g_ref, w_ref, isem, grads, osem,
    qt, kt, vt, dot, s_all, e_all, ot, sta, att, dqt, dkt, dvt,
    qb, kb, vb, db, eb, ob, sb,
    gb, send0, recv0, send1, recv1, send2, recv2, send3, recv3, send4, recv4, send5, recv5,
    ssem, rsem, pick_x, pick_y, pick_z,
    ogt, c_send, c_recv, a1_send, a1_recv, a2_send, a2_recv, b1_send, b1_recv, b2_send, b2_recv,
    z_send, z_recv, c_sem, a1_sem, a2_sem, b1_sem, b2_sem, z_sem,
):
    dp = lax.axis_index("dp")
    me = lax.axis_index("seq")
    my, mz, mx, mc = dp // NZ, dp % NZ, me // 2, me % 2
    half_rows = D // NY // 2
    wide_rows = up(half_rows, 128)
    z_rows = D // (NY * NZ)
    z_pad = up(z_rows, 16)

    loads = []
    for i, (src, dst) in enumerate(
        ((q_in, q_ref), (k_in, k_ref), (v_in, v_ref), (g_in, g_ref), (w_in, w_ref))
    ):
        loads.append(pltpu.make_async_copy(src, dst, isem.at[i]))
        loads[-1].start()

    barrier = pltpu.get_barrier_semaphore()
    for d in range(1, SPREAD):
        pl.semaphore_signal(
            barrier, inc=1, device_id=(dp, lax.rem(me + d, SPREAD)), device_id_type=MESH
        )
    for d in range(1, NY):
        pl.semaphore_signal(
            barrier, inc=1, device_id=(lax.rem(my + d, NY) * NZ + mz, me), device_id_type=MESH
        )
    for d in range(1, NZ):
        pl.semaphore_signal(
            barrier, inc=1, device_id=(my * NZ + lax.rem(mz + d, NZ), me), device_id_type=MESH
        )

    ends = []
    for i in range(SLIDES):
        ends.append(len_ref[0, i] if i == 0 else ends[-1] + len_ref[0, i])

    def exchange(kind, send, recv):
        copies = []
        for d in range(1, SPREAD):
            other = lax.rem(me + d, SPREAD)
            copies.append(
                pltpu.make_async_remote_copy(
                    src_ref=send.at[other],
                    dst_ref=recv.at[me],
                    send_sem=ssem.at[kind, d],
                    recv_sem=rsem.at[kind, d],
                    device_id=(dp, other),
                    device_id_type=MESH,
                )
            )
            copies[-1].start()
        return copies

    def arrive(kind, send, recv):
        for d in range(1, SPREAD):
            source = lax.rem(me + SPREAD - d, SPREAD)
            pltpu.make_async_remote_copy(
                src_ref=send.at[source],
                dst_ref=recv.at[source],
                send_sem=ssem.at[kind, d],
                recv_sem=rsem.at[kind, d],
                device_id=(dp, source),
                device_id_type=MESH,
            ).wait_recv()

    def along(size, place, device, send, recv, sem):
        def copy(d, slot, other):
            return pltpu.make_async_remote_copy(
                src_ref=send.at[other],
                dst_ref=recv.at[slot],
                send_sem=sem.at[0, d],
                recv_sem=sem.at[1, d],
                device_id=device(other),
                device_id_type=MESH,
            )

        def start():
            recv[place] = send[place]
            for d in range(1, size):
                copy(d, place, lax.rem(place + d, size)).start()

        def finish():
            for d in range(1, size):
                source = lax.rem(place + size - d, size)
                copy(d, source, source).wait_recv()

        def sent():
            for d in range(1, size):
                copy(d, place, lax.rem(place + d, size)).wait_send()

        return start, finish, sent

    def across(send, recv, sem):
        def copy(b, slot, other):
            return pltpu.make_async_remote_copy(
                src_ref=send.at[b],
                dst_ref=recv.at[slot],
                send_sem=sem.at[0, b],
                recv_sem=sem.at[1, slot],
                device_id=(dp, other),
                device_id_type=MESH,
            )

        def start():
            for b in range(NX):
                other = 4 * mc + b

                @pl.when(other != me)
                def _():
                    copy(b, mx, other).start()

                @pl.when(other == me)
                def _():
                    recv[mx] = send[b]

        def finish():
            for x in range(NX):
                source = 2 * x + me // 4

                @pl.when(source != me)
                def _():
                    copy(0, x, source).wait_recv()

        def sent():
            for b in range(NX):
                other = 4 * mc + b

                @pl.when(other != me)
                def _():
                    copy(b, mx, other).wait_send()

        return start, finish, sent

    def total(recv, count):
        out = recv[0].astype(F32)
        for i in range(1, count):
            out = out + recv[i].astype(F32)
        return out

    to = iota((SEG, SEG), 1)
    at = iota((SEG, SEG), 0)
    perm = jnp.where(at == to % CLS * SPREAD + to // CLS, 1.0, 0.0).astype(BF16)
    for i, (src, dst) in enumerate(((q_ref, qt), (k_ref, kt), (v_ref, vt))):
        loads[i].wait()
        dst[...] = mm_tn(src[...], perm).astype(BF16).reshape(NHEAD, DH, SEG)
    def class_rows(src, j):
        tile = pl.ds(j // 4 * 128, 128)
        both = jnp.concatenate([src[j, :, tile], src[j + SPREAD, :, tile]], 0)
        return both.astype(F32)

    for j in range(SPREAD):
        send0[j] = pack([class_rows(x, j) for x in (qt, kt, vt)], j, PACK3).astype(BF16)
    recv0[me] = send0[me]
    pl.semaphore_wait(barrier, SPREAD - 1 + NY - 1 + NZ - 1)
    copies = exchange(0, send0, recv0)

    loads[3].wait()
    ogt[...] = mm_tn(g_ref[...], perm).astype(BF16)
    loads[4].wait()
    dot[...] = mm(w_ref[...], ogt[...]).astype(BF16).reshape(NHEAD, DH, SEG)
    for j in range(SPREAD):
        send1[j] = pack([class_rows(dot, j)], j, PACK1).astype(BF16)
    recv1[me] = send1[me]
    copies += exchange(1, send1, recv1)
    pick_x[...] = pick_rows(NX, COLS, COLH, 128)
    pick_y[...] = pick_rows(NY, half_rows, COLH, wide_rows)
    pick_z[...] = pick_rows(NZ // 2, z_rows, wide_rows, z_pad)

    lane = iota((1, SEG), 1)
    k_mask, q_mask = mask_rows(me * SEG + lane % CLS * SPREAD + lane // CLS, ends)
    row = iota((PAD, SEG), 0)
    ones = jnp.where(row < 2, 1.0, 0.0).astype(BF16)

    def forward_s(h):
        s = scores(qt[h], kt[h], k_mask, q_mask)
        s_all[h] = s
        sta[h, 0:1] = jnp.max(s, 0, keepdims=True)

    def forward_o(h):
        e, o, top, lse = weigh(s_all[h], sta[h, 0:1], vt[h], ones)
        e_all[h] = e
        ot[h] = o
        att[pl.ds(pl.multiple_of(h * DH, 16), DH)] = o.astype(BF16)
        sta[h, 0:1] = top
        sta[h, 1:2] = lse
        sta[h, 2:3] = jnp.sum(dot[h].astype(F32) * o, 0, keepdims=True)

    def loop(body, first, last, unroll):
        def step(i, carry):
            for u in range(unroll):
                body(i * unroll + u)
            return carry

        lax.fori_loop(first // unroll, last // unroll, step, 0)

    loop(forward_s, 0, NHEAD, UF)
    loop(forward_o, 0, NHEAD, UF)

    narrow = lane_block(8)
    for j in range(SPREAD):
        tile = pl.ds(j // 4 * 128, 128)
        rows = jnp.concatenate(
            [sta[j, 1:2, tile], sta[j + SPREAD, 1:2, tile],
             sta[j, 2:3, tile], sta[j + SPREAD, 2:3, tile],
             jnp.zeros((4, 128), F32)], 0)
        send2[j] = shift(rows, -j)
    recv2[me] = send2[me]
    copies += exchange(2, send2, recv2)

    block = lane_block(PAIR)

    def gather(recv, dsts):
        for half in range(2):
            tile = pl.ds(half * 128, 128)
            outs = [jnp.zeros((PAIR, 128), F32)] * len(dsts)
            for s in range(half * 4, half * 4 + 4):
                got = recv[s].astype(F32)
                for t in range(len(dsts)):
                    outs[t] = jnp.where(block == s % 4, unpack(got, t, s), outs[t])
            for dst, out in zip(dsts, outs):
                out = out.astype(BF16)
                for u in range(2):
                    dst[u, :, tile] = out[u * DH : (u + 1) * DH]

    arrive(0, send0, recv0)
    gather(recv0, (qb, kb, vb))
    kb_mask, qb_mask = mask_rows(lane * SPREAD + me, ends)
    for u in range(2):
        e, o, top, lse = forward_head(qb[u], kb[u], vb[u], kb_mask, qb_mask, ones)
        eb[u] = e
        ob[u] = o
        sb[u, 0:1] = top
        sb[u, 1:2] = lse
    for s in range(SPREAD):
        tile = pl.ds(s // 4 * 128, 128)
        both = jnp.concatenate([ob[0, :, tile], ob[1, :, tile]], 0)
        send3[s] = pack([both], s, PACK1).astype(BF16)
    recv3[me] = send3[me]
    copies += exchange(3, send3, recv3)
    arrive(1, send1, recv1)
    gather(recv1, (db,))
    for u in range(2):
        sb[u, 2:3] = jnp.sum(db[u].astype(F32) * ob[u], 0, keepdims=True)
    for s in range(SPREAD):
        tile = pl.ds(s // 4 * 128, 128)
        rows = jnp.concatenate(
            [sb[0, 1:2, tile], sb[1, 1:2, tile], sb[0, 2:3, tile], sb[1, 2:3, tile],
             jnp.zeros((4, 128), F32)], 0)
        send4[s] = shift(rows, -s)
    recv4[me] = send4[me]
    copies += exchange(4, send4, recv4)

    arrive(4, send4, recv4)
    tall = iota((NHEAD, 128), 0)
    spot = lane_block(NHEAD)
    lse_b, delta_b = [], []
    for half in range(2):
        lb = jnp.full((NHEAD, 128), -1e30, F32)
        dbl = jnp.zeros((NHEAD, 128), F32)
        for j in range(half * 4, half * 4 + 4):
            x = shift(recv4[j], j)
            for u in range(2):
                here = (tall == j + SPREAD * u) & (spot == j % 4)
                lb = jnp.where(here, x[u : u + 1], lb)
                dbl = jnp.where(here, x[2 + u : 3 + u], dbl)
        lse_b.append(lb)
        delta_b.append(dbl)
    lse_b, delta_b = jnp.concatenate(lse_b, 1), jnp.concatenate(delta_b, 1)
    lse, w_a, w_b, delta = merge(sta[:, 1, :], sta[:, 2, :], lse_b, delta_b)
    sta[:, 2, :] = delta
    sta[:, 3, :] = jnp.exp2(sta[:, 0, :] - lse)
    arrive(3, send3, recv3)
    for j in range(SPREAD):
        other = unpack(recv3[j].astype(F32), 0, j)
        tile = slice(j // 4 * 128, j // 4 * 128 + 128)
        for u in range(2):
            h = j + SPREAD * u
            mine = ot[h, :, tile]
            both = mine * w_a[h : h + 1, tile] + other[u * DH : (u + 1) * DH] * w_b[h : h + 1, tile]
            x = jnp.where(lane_block(DH) == j % 4, both, mine)
            att[h * DH : (h + 1) * DH, tile] = x.astype(BF16)

    def part(which, side):
        rows = [
            att[y * 2 * half_rows + which * half_rows : y * 2 * half_rows + (which + 1) * half_rows]
            for y in range(NY)
        ]
        rows = jnp.concatenate(rows, 0)
        if which == 0:
            return mm_nt(rows, ogt[pl.ds(pl.multiple_of(side * COLH, 128), COLH)])
        return mm_nt(ogt[pl.ds(pl.multiple_of(side * COLH, 128), COLH)], rows)

    sibling = [
        pltpu.make_async_remote_copy(
            src_ref=c_send.at[i],
            dst_ref=c_recv.at[i],
            send_sem=c_sem.at[0, i],
            recv_sem=c_sem.at[1, i],
            device_id=(dp, 2 * mx + 1 - mc),
            device_id_type=MESH,
        )
        for i in range(2)
    ]
    for i in range(2):
        c_send[i] = part(i, 1 - mc).astype(BF16)
        sibling[i].start()
    a1 = along(NY, my, lambda y: (y * NZ + mz, me), a1_send, a1_recv, a1_sem)
    a2 = across(a2_send, a2_recv, a2_sem)
    b1 = across(b1_send, b1_recv, b1_sem)
    b2 = along(NY, my, lambda y: (y * NZ + mz, me), b2_send, b2_recv, b2_sem)
    zz = along(NZ, mz, lambda z: (my * NZ + z, me), z_send, z_recv, z_sem)

    def step_a():
        for i, (send, count, step) in enumerate(((a1_send, NY, a1), (a2_send, NX, a2))):
            own = part(i, mc)
            sibling[i].wait_recv()
            own = (own + c_recv[i].astype(F32)).astype(BF16)
            for n in range(count):
                send[n] = own[n * COLH // count : (n + 1) * COLH // count]
            step[0]()

    def step_b():
        a1[1]()
        x = total(a1_recv, NY).astype(BF16)
        x = mm_nt(x, pick_x[...]).astype(BF16)
        for b in range(NX):
            b1_send[b] = x[:, b * 128 : (b + 1) * 128]
        b1[0]()
        a2[1]()
        x = total(a2_recv, NX).astype(BF16)
        x = mm_nt(x, pick_y[...]).astype(BF16)
        for y in range(NY):
            b2_send[y] = x[:, y * wide_rows : (y + 1) * wide_rows]
        b2[0]()

    def step_z():
        b1[1]()
        x = total(b1_recv, NX)
        x = jnp.concatenate([x, jnp.zeros((wide_rows - half_rows, 128), F32)], 0)
        x = mm(pick_z[...], x.astype(BF16)).astype(BF16)
        for z in range(NZ // 2):
            z_send[z] = x[z * z_pad : (z + 1) * z_pad]
        b2[1]()
        x = total(b2_recv, NY)
        x = jnp.concatenate([x, jnp.zeros((128 - COLS, wide_rows), F32)], 0)
        x = mm_nt(pick_z[...], x.astype(BF16)).astype(BF16)
        for z in range(NZ // 2):
            z_send[NZ // 2 + z] = x[z * z_pad : (z + 1) * z_pad]
        zz[0]()

    def finish():
        zz[1]()
        dw_ref[...] = total(z_recv, NZ)

    arrive(2, send2, recv2)
    halves = []
    for half in range(2):
        out = jnp.zeros((8, 128), F32)
        for s in range(half * 4, half * 4 + 4):
            out = jnp.where(narrow == s % 4, shift(recv2[s], s), out)
        halves.append(out)
    theirs = jnp.concatenate(halves, 1)
    for u in range(2):
        top = sb[u, 0:1]
        lse, _, _, delta = merge(theirs[u : u + 1], theirs[2 + u : 3 + u], sb[u, 1:2], sb[u, 2:3])
        grads_b = backward_head(
            qb[u], kb[u], vb[u], db[u], eb[u], ones, jnp.exp2(top - lse), delta
        )
        for t in range(3):
            gb[t, u * DH : (u + 1) * DH] = grads_b[t]
    for s in range(SPREAD):
        tile = pl.ds(s // 4 * 128, 128)
        send5[s] = pack([gb[t, :, tile] for t in range(3)], s, PACK3).astype(BF16)
    recv5[me] = send5[me]

    def backward(h):
        dq, dk, dv = backward_head(
            qt[h], kt[h], vt[h], dot[h], e_all[h], ones, sta[h, 3:4], sta[h, 2:3]
        )
        dqt[h] = dq
        dkt[h] = dk
        dvt[h] = dv

    step_a()
    copies += exchange(5, send5, recv5)
    loop(backward, 0, NHEAD // 2, UB)
    step_b()
    loop(backward, NHEAD // 2, NHEAD, UB)
    step_z()

    arrive(5, send5, recv5)
    for j in range(SPREAD):
        tile = pl.ds(j // 4 * 128, 128)
        got = recv5[j].astype(F32)
        for t, dst in enumerate((dqt, dkt, dvt)):
            part = jnp.where(block == j % 4, unpack(got, t, j), 0.0)
            for u in range(2):
                h = j + SPREAD * u
                dst[h, :, tile] = dst[h, :, tile] + part[u * DH : (u + 1) * DH]
    stores = []
    for t, src in enumerate((dqt, dkt, dvt)):
        grads[t] = mm_nt(perm, src[...].reshape(D, SEG).astype(BF16)).astype(BF16)
        stores.append(pltpu.make_async_copy(grads.at[t], grads_ref.at[t], osem.at[t]))
        stores[-1].start()

    finish()
    for c in stores:
        c.wait()
    for c in copies + sibling:
        c.wait_send()
    for step in (a1, a2, b1, b2, zz):
        step[2]()


def final_kernel(grads_ref, part_ref, dq_ref, dk_ref, dv_ref, dw_ref, x, isem, osem):
    loads = [pltpu.make_async_copy(grads_ref.at[t], x.at[t], isem.at[t]) for t in range(3)]
    for c in loads:
        c.start()
    dw_ref[...] = part_ref[0 : dw_ref.shape[0], 0 : dw_ref.shape[1]]
    stores = []
    for t, dst in enumerate((dq_ref, dk_ref, dv_ref)):
        loads[t].wait()
        stores.append(pltpu.make_async_copy(x.at[t], dst, osem.at[t]))
        stores[-1].start()
    for c in stores:
        c.wait()


def on_device(queries, keys, values, out_grad, out_weight, slide_lengths):
    vmem = pl.BlockSpec(memory_space=pltpu.VMEM)
    heads = lambda n, dtype: pltpu.VMEM((n, DH, SEG), dtype)
    half_rows = D // NY // 2
    wide_rows = up(half_rows, 128)
    z_rows = D // (NY * NZ)
    z_pad = up(z_rows, 16)
    grads, partial = pl.pallas_call(
        kernel,
        out_shape=(
            jax.ShapeDtypeStruct((3, SEG, D), BF16),
            jax.ShapeDtypeStruct((z_pad, 128), F32),
        ),
        in_specs=[pl.BlockSpec(memory_space=pl.ANY)] * 5 + [pl.BlockSpec(memory_space=pltpu.SMEM)],
        out_specs=(pl.BlockSpec(memory_space=pl.ANY), vmem),
        scratch_shapes=[
            pltpu.VMEM((SEG, D), BF16), pltpu.VMEM((SEG, D), BF16), pltpu.VMEM((SEG, D), BF16),
            pltpu.VMEM((SEG, D), BF16), pltpu.VMEM((D, D), BF16),
            pltpu.SemaphoreType.DMA((5,)),
            pltpu.VMEM((3, SEG, D), BF16),
            pltpu.SemaphoreType.DMA((3,)),
            heads(NHEAD, BF16), heads(NHEAD, BF16), heads(NHEAD, BF16), heads(NHEAD, BF16),
            pltpu.VMEM((NHEAD, SEG, SEG), F32),
            pltpu.VMEM((NHEAD, SEG, SEG), BF16),
            heads(NHEAD, F32),
            pltpu.VMEM((NHEAD, 8, SEG), F32),
            pltpu.VMEM((D, SEG), BF16),
            heads(NHEAD, F32), heads(NHEAD, F32), heads(NHEAD, F32),
            heads(2, BF16), heads(2, BF16), heads(2, BF16), heads(2, BF16),
            pltpu.VMEM((2, SEG, SEG), BF16),
            heads(2, F32),
            pltpu.VMEM((2, 8, SEG), F32),
            pltpu.VMEM((3, PAIR, SEG), F32),
            *[
                pltpu.VMEM((SPREAD, rows, 128), dtype)
                for rows, dtype in (
                    (PACK3, BF16), (PACK1, BF16), (8, F32), (PACK1, BF16), (8, F32), (PACK3, BF16)
                )
                for _ in range(2)
            ],
            pltpu.SemaphoreType.DMA((6, SPREAD)),
            pltpu.SemaphoreType.DMA((6, SPREAD)),
            pltpu.VMEM((NX * 128, COLH), BF16),
            pltpu.VMEM((NY * wide_rows, COLH), BF16),
            pltpu.VMEM((NZ // 2 * z_pad, wide_rows), BF16),
            pltpu.VMEM((D, SEG), BF16),
            pltpu.VMEM((2, COLH, COLH), BF16), pltpu.VMEM((2, COLH, COLH), BF16),
            pltpu.VMEM((NY, half_rows, COLH), BF16), pltpu.VMEM((NY, half_rows, COLH), BF16),
            pltpu.VMEM((NX, COLS, COLH), BF16), pltpu.VMEM((NX, COLS, COLH), BF16),
            pltpu.VMEM((NX, half_rows, 128), BF16), pltpu.VMEM((NX, half_rows, 128), BF16),
            pltpu.VMEM((NY, COLS, wide_rows), BF16), pltpu.VMEM((NY, COLS, wide_rows), BF16),
            pltpu.VMEM((NZ, z_pad, 128), BF16), pltpu.VMEM((NZ, z_pad, 128), BF16),
            pltpu.SemaphoreType.DMA((2, 2)),
            pltpu.SemaphoreType.DMA((2, NY)), pltpu.SemaphoreType.DMA((2, NX)),
            pltpu.SemaphoreType.DMA((2, NX)), pltpu.SemaphoreType.DMA((2, NY)),
            pltpu.SemaphoreType.DMA((2, NZ)),
        ],
        compiler_params=pltpu.CompilerParams(
            collective_id=0, has_side_effects=True, vmem_limit_bytes=VMEM_LIMIT
        ),
    )(queries, keys, values, out_grad, out_weight, slide_lengths)
    out = jax.ShapeDtypeStruct((SEG, D), BF16)
    return pl.pallas_call(
        final_kernel,
        out_shape=(out, out, out, jax.ShapeDtypeStruct((z_rows, COLS), F32)),
        in_specs=[pl.BlockSpec(memory_space=pl.ANY), vmem],
        out_specs=(pl.BlockSpec(memory_space=pl.ANY),) * 3 + (vmem,),
        scratch_shapes=[
            pltpu.VMEM((3, SEG, D), BF16),
            pltpu.SemaphoreType.DMA((3,)),
            pltpu.SemaphoreType.DMA((3,)),
        ],
        compiler_params=pltpu.CompilerParams(vmem_limit_bytes=VMEM_LIMIT),
    )(grads, partial)


def solution(mesh):
    placed = (
        P(("dp", "seq"), None),
        P(("dp", "seq"), None),
        P(("dp", "seq"), None),
        P(("dp", "seq"), None),
        P(),
        P("dp", None),
    )
    return jax.shard_map(
        on_device,
        mesh=mesh,
        in_specs=placed,
        out_specs=(
            P(("dp", "seq"), None),
            P(("dp", "seq"), None),
            P(("dp", "seq"), None),
            P("dp", "seq"),
        ),
        check_vma=False,
    )
```

```python
import functools

import jax
import jax.numpy as jnp
from jax import lax
from jax.experimental import pallas as pl
from jax.experimental.pallas import tpu as pltpu
from jax.sharding import PartitionSpec as P

MESH = pl.DeviceIdType.MESH
NHEAD = 16
DH = 48
D = NHEAD * DH
SEG = 256
SPREAD = 8
CLS = SEG // SPREAD
PAIR = 2 * DH
DENSE = PAIR // 4
PACK1 = 32
PACK3 = 80
SLIDES = 4
NX = 4
UF = 8
UB = 8
NY = 4
NZ = 16
COLS = D // SPREAD
COLH = D // 2
MAIN = 128
REM = D // NY - MAIN
DROWS = COLS + COLS // 2
PAD = 16
BIG = 2.0**20
VMEM_LIMIT = 60 * 1024 * 1024
LOG2E = 1.4426950408889634
SCALE = DH**-0.5
F32 = jnp.float32
BF16 = jnp.bfloat16


def iota(shape, dim):
    return lax.broadcasted_iota(jnp.int32, shape, dim)


def mm(a, b):
    return jnp.dot(a, b, preferred_element_type=F32)


def mm_tn(a, b):
    return lax.dot_general(a, b, (((0,), (0,)), ((), ())), preferred_element_type=F32)


def mm_nt(a, b):
    return lax.dot_general(a, b, (((1,), (1,)), ((), ())), preferred_element_type=F32)


def mask_rows(pos, ends):
    row = iota((PAD, pos.shape[1]), 0)
    starts = [0] + ends[:-1]
    hit = jnp.zeros((PAD, pos.shape[1]), F32)
    for i in range(SLIDES):
        inside = jnp.where((pos >= starts[i]) & (pos < ends[i]), 1.0, 0.0)
        hit = jnp.where(row == i, inside, hit)
    off = jnp.where(row < SLIDES, (hit - 1.0) * BIG, 0.0)
    return hit.astype(BF16), off.astype(BF16)


def scores(qt, kt, k_mask, q_mask):
    return mm_tn(jnp.concatenate([kt, k_mask], 0), jnp.concatenate([qt, q_mask], 0))


def weigh(s, top, vt, ones):
    top = top * (SCALE * LOG2E)
    e = jnp.exp2(s * (SCALE * LOG2E) - top).astype(BF16)
    ov = mm(jnp.concatenate([vt, ones], 0), e)
    total = ov[DH : DH + 1]
    return e, ov[:DH] * (1.0 / total), top, top + jnp.log(total) * LOG2E


def forward_head(qt, kt, vt, k_mask, q_mask, ones):
    s = scores(qt, kt, k_mask, q_mask)
    return weigh(s, jnp.max(s, 0, keepdims=True), vt, ones)


def backward_head(qt, kt, vt, dot, e, ones, ratio, delta):
    hi = delta.astype(BF16)
    lo = (delta - hi.astype(F32)).astype(BF16)
    row = iota((PAD, delta.shape[1]), 0)
    less = jnp.where(row == 0, -hi.astype(F32), jnp.where(row == 1, -lo.astype(F32), 0.0))
    dp = mm_tn(jnp.concatenate([vt, ones], 0), jnp.concatenate([dot, less.astype(BF16)], 0))
    g = (e.astype(F32) * dp).astype(BF16)
    dv = mm_nt((dot.astype(F32) * ratio).astype(BF16), e)
    ratio = ratio * SCALE
    dk = mm_nt((qt.astype(F32) * ratio).astype(BF16), g)
    dq = mm(kt, g) * ratio
    return dq, dk, dv


def blend(lse_a, lse_b):
    top = jnp.maximum(lse_a, lse_b)
    lse = top + jnp.log(jnp.exp2(lse_a - top) + jnp.exp2(lse_b - top)) * LOG2E
    return lse, jnp.exp2(lse_a - lse), jnp.exp2(lse_b - lse)


def three_terms(x):
    out = []
    for _ in range(3):
        out.append(x.astype(BF16).astype(F32))
        x = x - out[-1]
    return jnp.concatenate(out + [jnp.zeros((5, x.shape[1]), F32)], 0)


def lane_block(rows):
    return iota((rows, 128), 1) // CLS


def up(n, to):
    return (n + to - 1) // to * to


def far_first(size):
    return sorted(range(1, size), key=lambda d: -min(d, size - d))


def shift(x, blocks):
    blocks = blocks % 4
    return x if blocks == 0 else pltpu.roll(x, blocks * CLS, 1)


def pack(parts, j, rows):
    out = []
    block = lane_block(DENSE)
    for x in parts:
        dense = jnp.zeros((DENSE, 128), F32)
        for b in range(4):
            dense = jnp.where(block == b, shift(x[b * DENSE : (b + 1) * DENSE], b - j), dense)
        out.append(dense)
    if rows > len(parts) * DENSE:
        out.append(jnp.zeros((rows - len(parts) * DENSE, 128), F32))
    return jnp.concatenate(out, 0)


def unpack(x, t, j):
    x = x[t * DENSE : (t + 1) * DENSE]
    return jnp.concatenate([shift(x, j - b) for b in range(4)], 0)


def kernel(
    q_in, k_in, v_in, g_in, w_in, len_ref,
    grads_ref, dw_ref,
    q_ref, k_ref, v_ref, g_ref, w_ref, isem, grads, osem,
    qt, kt, vt, dot, s_all, e_all, ot, sta, att, dqt, dkt, dvt,
    qb, kb, vb, db, eb, ob, sb,
    gb, send0, recv0, send1, recv1, send2, recv2, send3, recv3, send4, recv4, send5, recv5,
    ssem, rsem, pick_main, pick_rest,
    ogt, att_x, lse_own, lse_x, og_x,
    d_send, d_recv, z_send, z_recv, c_sem, d_sem, z_sem,
):
    dp = lax.axis_index("dp")
    me = lax.axis_index("seq")
    my, mz, mx, mc = dp // NZ, dp % NZ, me // 2, me % 2
    z_rows = D // (NY * NZ)
    z_pad = up(z_rows, 16)

    loads = []
    for i, (src, dst) in enumerate(
        ((q_in, q_ref), (k_in, k_ref), (v_in, v_ref), (g_in, g_ref), (w_in, w_ref))
    ):
        loads.append(pltpu.make_async_copy(src, dst, isem.at[i]))
    for c in loads[:3]:
        c.start()

    barrier = pltpu.get_barrier_semaphore()
    for d in far_first(NZ):
        pl.semaphore_signal(
            barrier, inc=1, device_id=(my * NZ + lax.rem(mz + d, NZ), me), device_id_type=MESH
        )
    for d in range(1, NY):
        for x in range(NX):
            other = (lax.rem(my + d, NY) * NZ + mz, 2 * x + me // 4)
            pl.semaphore_signal(barrier, inc=1, device_id=other, device_id_type=MESH)
    for d in range(1, SPREAD):
        pl.semaphore_signal(
            barrier, inc=1, device_id=(dp, lax.rem(me + d, SPREAD)), device_id_type=MESH
        )

    ends = []
    for i in range(SLIDES):
        ends.append(len_ref[0, i] if i == 0 else ends[-1] + len_ref[0, i])

    def exchange(kind, send, recv, group=1):
        copies = []
        for d in far_first(SPREAD):
            other = lax.rem(me + d, SPREAD)
            copies.append(
                pltpu.make_async_remote_copy(
                    src_ref=send.at[other // group],
                    dst_ref=recv.at[me],
                    send_sem=ssem.at[kind, d],
                    recv_sem=rsem.at[kind, d],
                    device_id=(dp, other),
                    device_id_type=MESH,
                )
            )
            copies[-1].start()
        return copies

    def arrive(kind, send, recv, group=1):
        for d in range(1, SPREAD):
            source = lax.rem(me + SPREAD - d, SPREAD)
            pltpu.make_async_remote_copy(
                src_ref=send.at[source // group],
                dst_ref=recv.at[source],
                send_sem=ssem.at[kind, d],
                recv_sem=rsem.at[kind, d],
                device_id=(dp, source),
                device_id_type=MESH,
            ).wait_recv()

    def along(size, place, device, send, recv, sem):
        def copy(d, slot, other):
            return pltpu.make_async_remote_copy(
                src_ref=send.at[other],
                dst_ref=recv.at[slot],
                send_sem=sem.at[0, d],
                recv_sem=sem.at[1, d],
                device_id=device(other),
                device_id_type=MESH,
            )

        def start():
            for d in far_first(size):
                copy(d, place, lax.rem(place + d, size)).start()
            recv[place] = send[place]

        def finish():
            for d in range(1, size):
                source = lax.rem(place + size - d, size)
                copy(d, source, source).wait_recv()

        def sent():
            for d in range(1, size):
                copy(d, place, lax.rem(place + d, size)).wait_send()

        return start, finish, sent

    def plane_each(do, own=None):
        for d in (2, 1, 3, 0):
            y = lax.rem(my + d, NY)
            for b in range(NX):
                other = 4 * mc + b
                copy = pltpu.make_async_remote_copy(
                    src_ref=d_send.at[y * NX + b],
                    dst_ref=d_recv.at[d * NX + mx],
                    send_sem=d_sem.at[0, d * NX + b],
                    recv_sem=d_sem.at[1, d * NX + mx],
                    device_id=(y * NZ + mz, other),
                    device_id_type=MESH,
                )
                if d:
                    do(copy)
                else:
                    pl.when(other != me)(functools.partial(do, copy))
                    if own is not None:
                        pl.when(other == me)(functools.partial(own, b))

    def plane_own(b):
        d_recv[mx] = d_send[my * NX + b]

    def plane_arrive():
        for d in (0, 1, 3, 2):
            y = lax.rem(my + NY - d, NY)
            for x in range(NX):
                source = 2 * x + me // 4
                copy = pltpu.make_async_remote_copy(
                    src_ref=d_send.at[0],
                    dst_ref=d_recv.at[d * NX + x],
                    send_sem=d_sem.at[0, d * NX],
                    recv_sem=d_sem.at[1, d * NX + x],
                    device_id=(y * NZ + mz, source),
                    device_id_type=MESH,
                )
                if d:
                    copy.wait_recv()
                else:
                    pl.when(source != me)(copy.wait_recv)

    def total(recv, count):
        out = recv[0].astype(F32)
        for i in range(1, count):
            out = out + recv[i].astype(F32)
        return out

    to = iota((SEG, SEG), 1)
    at = iota((SEG, SEG), 0)
    perm = jnp.where(at == to % CLS * SPREAD + to // CLS, 1.0, 0.0).astype(BF16)
    for i, (src, dst) in enumerate(((q_ref, qt), (k_ref, kt), (v_ref, vt))):
        loads[i].wait()
        if i == 0:
            loads[3].start()
            loads[4].start()
        dst[...] = mm_tn(src[...], perm).astype(BF16).reshape(NHEAD, DH, SEG)
    def class_rows(src, j):
        tile = pl.ds(j // 4 * 128, 128)
        both = jnp.concatenate([src[j, :, tile], src[j + SPREAD, :, tile]], 0)
        return both.astype(F32)

    for j in range(SPREAD):
        send0[j] = pack([class_rows(x, j) for x in (qt, kt, vt)], j, PACK3).astype(BF16)
    recv0[me] = send0[me]
    pl.semaphore_wait(barrier, SPREAD - 1 + (NY - 1) * NX + NZ - 1)
    copies = exchange(0, send0, recv0)

    loads[3].wait()
    ogt[...] = mm_tn(g_ref[...], perm).astype(BF16)
    loads[4].wait()
    dot[...] = mm(w_ref[...], ogt[...]).astype(BF16).reshape(NHEAD, DH, SEG)
    for j in range(SPREAD):
        send1[j] = pack([class_rows(dot, j)], j, PACK1).astype(BF16)
    recv1[me] = send1[me]
    copies += exchange(1, send1, recv1)
    z_at = iota((NZ * z_pad, 128), 0)
    lane = iota((NZ * z_pad, 128), 1)
    z_at = jnp.where(z_at % z_pad < z_rows, z_at // z_pad * z_rows + z_at % z_pad, -1)
    pick_main[...] = jnp.where(lane == z_at, 1.0, 0.0).astype(BF16)
    pick_rest[...] = jnp.where(lane + MAIN == z_at, 1.0, 0.0).astype(BF16)

    lane = iota((1, SEG), 1)
    k_mask, q_mask = mask_rows(me * SEG + lane % CLS * SPREAD + lane // CLS, ends)
    row = iota((PAD, SEG), 0)
    ones = jnp.where(row < 2, 1.0, 0.0).astype(BF16)

    def forward_s(h):
        s = scores(qt[h], kt[h], k_mask, q_mask)
        s_all[h] = s
        sta[h, 0:1] = jnp.max(s, 0, keepdims=True)

    def forward_o(h):
        e, o, top, lse = weigh(s_all[h], sta[h, 0:1], vt[h], ones)
        e_all[h] = e
        ot[h] = o
        att[pl.ds(pl.multiple_of(h * DH, 16), DH)] = o.astype(BF16)
        sta[h, 0:1] = top
        sta[h, 1:2] = lse
        sta[h, 2:3] = jnp.sum(dot[h].astype(F32) * o, 0, keepdims=True)

    def loop(body, first, last, unroll):
        def step(i, carry):
            for u in range(unroll):
                body(i * unroll + u)
            return carry

        lax.fori_loop(first // unroll, last // unroll, step, 0)

    loop(forward_s, 0, NHEAD, UF)
    loop(forward_o, 0, NHEAD, UF)

    lse_own[...] = sta[:, 1, :]
    early = [
        (att, att_x),
        (lse_own, lse_x),
        (ogt.at[pl.ds(pl.multiple_of((1 - mc) * COLH, 128), COLH)], og_x),
    ]
    sibling = [
        pltpu.make_async_remote_copy(
            src_ref=src,
            dst_ref=dst,
            send_sem=c_sem.at[0, i],
            recv_sem=c_sem.at[1, i],
            device_id=(dp, 2 * mx + 1 - mc),
            device_id_type=MESH,
        )
        for i, (src, dst) in enumerate(early)
    ]
    for c in sibling:
        c.start()

    narrow = lane_block(8)
    for j in range(SPREAD):
        tile = pl.ds(j // 4 * 128, 128)
        rows = jnp.concatenate(
            [sta[j, 1:2, tile], sta[j + SPREAD, 1:2, tile],
             sta[j, 2:3, tile], sta[j + SPREAD, 2:3, tile],
             jnp.zeros((4, 128), F32)], 0)
        send2[j] = shift(rows, -j)
    recv2[me] = send2[me]
    copies += exchange(2, send2, recv2)

    block = lane_block(PAIR)

    def gather(recv, dsts):
        for half in range(2):
            tile = pl.ds(half * 128, 128)
            outs = [jnp.zeros((PAIR, 128), F32)] * len(dsts)
            for s in range(half * 4, half * 4 + 4):
                got = recv[s].astype(F32)
                for t in range(len(dsts)):
                    outs[t] = jnp.where(block == s % 4, unpack(got, t, s), outs[t])
            for dst, out in zip(dsts, outs):
                out = out.astype(BF16)
                for u in range(2):
                    dst[u, :, tile] = out[u * DH : (u + 1) * DH]

    arrive(0, send0, recv0)
    gather(recv0, (qb, kb, vb))
    kb_mask, qb_mask = mask_rows(lane * SPREAD + me, ends)
    for u in range(2):
        e, o, top, lse = forward_head(qb[u], kb[u], vb[u], kb_mask, qb_mask, ones)
        eb[u] = e
        ob[u] = o
        sb[u, 0:1] = top
        sb[u, 1:2] = lse
    for s in range(SPREAD):
        tile = pl.ds(s // 4 * 128, 128)
        both = jnp.concatenate([ob[0, :, tile], ob[1, :, tile]], 0)
        lses = jnp.where(
            lane_block(1) == 0, shift(sb[0, 1:2, tile], -s), shift(sb[1, 1:2, tile], 1 - s)
        )
        dense = jnp.concatenate([pack([both], s, DENSE), three_terms(lses)], 0)
        send3[s // 2, s % 2] = dense.astype(BF16)
    recv3[me] = send3[mx]
    copies += exchange(3, send3, recv3, 2)
    arrive(1, send1, recv1)
    gather(recv1, (db,))
    for u in range(2):
        sb[u, 2:3] = jnp.sum(db[u].astype(F32) * ob[u], 0, keepdims=True)
    for s in range(SPREAD):
        tile = pl.ds(s // 4 * 128, 128)
        rows = jnp.concatenate([sb[0, 2:3, tile], sb[1, 2:3, tile], jnp.zeros((6, 128), F32)], 0)
        send4[s] = shift(rows, -s)
    recv4[me] = send4[me]
    copies += exchange(4, send4, recv4)

    tall = iota((NHEAD, 128), 0)
    spot = lane_block(NHEAD)

    def spread_rows(pairs, empty):
        sides = []
        for half in range(2):
            out = jnp.full((NHEAD, 128), empty, F32)
            for j in range(half * 4, half * 4 + 4):
                for u in range(2):
                    here = (tall == j + SPREAD * u) & (spot == j % 4)
                    out = jnp.where(here, pairs[j][u], out)
            sides.append(out)
        return jnp.concatenate(sides, 1)

    def combine(which, lse_a, target):
        got = [recv3[j, which].astype(F32) for j in range(SPREAD)]
        pairs = []
        for j in range(SPREAD):
            x = got[j][DENSE : DENSE + 1] + got[j][DENSE + 1 : DENSE + 2]
            x = x + got[j][DENSE + 2 : DENSE + 3]
            pairs.append((shift(x, j), shift(x, j - 1)))
        lse, w_a, w_b = blend(lse_a, spread_rows(pairs, -1e30))
        for j in range(SPREAD):
            other = unpack(got[j], 0, j)
            tile = slice(j // 4 * 128, j // 4 * 128 + 128)
            for u in range(2):
                h = j + SPREAD * u
                mine = target[h * DH : (h + 1) * DH, tile].astype(F32)
                both = mine * w_a[h : h + 1, tile]
                both = both + other[u * DH : (u + 1) * DH] * w_b[h : h + 1, tile]
                x = jnp.where(lane_block(DH) == j % 4, both, mine)
                target[h * DH : (h + 1) * DH, tile] = x.astype(BF16)
        return lse, w_a, w_b

    for c in sibling:
        c.wait()
    arrive(3, send3, recv3, 2)
    lse, w_a, w_b = combine(mc, lse_own[...], att)
    combine(1 - mc, lse_x[...], att_x)

    def part(first, count):
        out = 0.0
        for rows, cols in (
            (att, ogt.at[pl.ds(pl.multiple_of(mc * COLH, 128), COLH)]),
            (att_x, og_x),
        ):
            starts = [y * (MAIN + REM) + first for y in range(NY)]
            x = jnp.concatenate([rows[i : i + count] for i in starts], 0)
            out = out + mm_nt(cols[...], x)
        return out

    zz = along(NZ, mz, lambda z: (my * NZ + z, me), z_send, z_recv, z_sem)
    main, rest = part(0, MAIN), part(MAIN, REM)
    low = iota((COLS // 2, 128), 1) < REM
    for y in range(NY):
        for b in range(NX):
            d_send[y * NX + b, :COLS] = main[
                b * COLS : (b + 1) * COLS, y * MAIN : (y + 1) * MAIN
            ].astype(BF16)
            x = rest[b * COLS : (b + 1) * COLS, y // 2 * 128 : y // 2 * 128 + 128]
            top, bottom = x[: COLS // 2], x[COLS // 2 :]
            if y % 2:
                top = pltpu.roll(top, REM, 1)
            else:
                bottom = pltpu.roll(bottom, REM, 1)
            d_send[y * NX + b, COLS:] = jnp.where(low, top, bottom).astype(BF16)
    plane_each(lambda copy: copy.start(), plane_own)

    arrive(4, send4, recv4)
    pairs = []
    for j in range(SPREAD):
        x = shift(recv4[j], j)
        pairs.append((x[0:1], x[1:2]))
    sta[:, 2, :] = w_a * sta[:, 2, :] + w_b * spread_rows(pairs, 0.0)
    sta[:, 3, :] = jnp.exp2(sta[:, 0, :] - lse)

    def step_z():
        plane_arrive()
        x = total(d_recv, NY * NX)
        rest = jnp.concatenate([x[COLS:], pltpu.roll(x[COLS:], REM, 1)], 0)
        pad = jnp.zeros((128 - COLS, 128), F32)
        x = jnp.concatenate([x[:COLS], pad], 0).astype(BF16)
        rest = jnp.concatenate([rest, pad], 0).astype(BF16)
        x = (mm_nt(pick_main[...], x) + mm_nt(pick_rest[...], rest)).astype(BF16)
        for z in range(NZ):
            z_send[z] = x[z * z_pad : (z + 1) * z_pad]
        zz[0]()

    def finish():
        zz[1]()
        dw_ref[...] = total(z_recv, NZ)

    arrive(2, send2, recv2)
    halves = []
    for half in range(2):
        out = jnp.zeros((8, 128), F32)
        for s in range(half * 4, half * 4 + 4):
            out = jnp.where(narrow == s % 4, shift(recv2[s], s), out)
        halves.append(out)
    theirs = jnp.concatenate(halves, 1)
    for u in range(2):
        top = sb[u, 0:1]
        lse, w_a, w_b = blend(theirs[u : u + 1], sb[u, 1:2])
        delta = w_a * theirs[2 + u : 3 + u] + w_b * sb[u, 2:3]
        grads_b = backward_head(
            qb[u], kb[u], vb[u], db[u], eb[u], ones, jnp.exp2(top - lse), delta
        )
        for t in range(3):
            gb[t, u * DH : (u + 1) * DH] = grads_b[t]
    for s in range(SPREAD):
        tile = pl.ds(s // 4 * 128, 128)
        send5[s] = pack([gb[t, :, tile] for t in range(3)], s, PACK3).astype(BF16)
    recv5[me] = send5[me]

    def backward(h):
        dq, dk, dv = backward_head(
            qt[h], kt[h], vt[h], dot[h], e_all[h], ones, sta[h, 3:4], sta[h, 2:3]
        )
        dqt[h] = dq
        dkt[h] = dk
        dvt[h] = dv

    copies += exchange(5, send5, recv5)
    loop(backward, 0, NHEAD, UB)
    step_z()

    arrive(5, send5, recv5)
    for j in range(SPREAD):
        tile = pl.ds(j // 4 * 128, 128)
        got = recv5[j].astype(F32)
        for t, dst in enumerate((dqt, dkt, dvt)):
            part = jnp.where(block == j % 4, unpack(got, t, j), 0.0)
            for u in range(2):
                h = j + SPREAD * u
                dst[h, :, tile] = dst[h, :, tile] + part[u * DH : (u + 1) * DH]
    stores = []
    for t, src in enumerate((dqt, dkt, dvt)):
        grads[t] = mm_nt(perm, src[...].reshape(D, SEG).astype(BF16)).astype(BF16)
        stores.append(pltpu.make_async_copy(grads.at[t], grads_ref.at[t], osem.at[t]))
        stores[-1].start()

    finish()
    for c in stores:
        c.wait()
    for c in copies:
        c.wait_send()
    plane_each(lambda copy: copy.wait_send())
    zz[2]()


def final_kernel(grads_ref, part_ref, dq_ref, dk_ref, dv_ref, dw_ref, x, isem, osem):
    loads = [pltpu.make_async_copy(grads_ref.at[t], x.at[t], isem.at[t]) for t in range(3)]
    for c in loads:
        c.start()
    dw_ref[...] = part_ref[0 : dw_ref.shape[0], 0 : dw_ref.shape[1]]
    stores = []
    for t, dst in enumerate((dq_ref, dk_ref, dv_ref)):
        loads[t].wait()
        stores.append(pltpu.make_async_copy(x.at[t], dst, osem.at[t]))
        stores[-1].start()
    for c in stores:
        c.wait()


def on_device(queries, keys, values, out_grad, out_weight, slide_lengths):
    vmem = pl.BlockSpec(memory_space=pltpu.VMEM)
    heads = lambda n, dtype: pltpu.VMEM((n, DH, SEG), dtype)
    z_rows = D // (NY * NZ)
    z_pad = up(z_rows, 16)
    grads, partial = pl.pallas_call(
        kernel,
        out_shape=(
            jax.ShapeDtypeStruct((3, SEG, D), BF16),
            jax.ShapeDtypeStruct((z_pad, 128), F32),
        ),
        in_specs=[pl.BlockSpec(memory_space=pl.ANY)] * 5 + [pl.BlockSpec(memory_space=pltpu.SMEM)],
        out_specs=(pl.BlockSpec(memory_space=pl.ANY), vmem),
        scratch_shapes=[
            pltpu.VMEM((SEG, D), BF16), pltpu.VMEM((SEG, D), BF16), pltpu.VMEM((SEG, D), BF16),
            pltpu.VMEM((SEG, D), BF16), pltpu.VMEM((D, D), BF16),
            pltpu.SemaphoreType.DMA((5,)),
            pltpu.VMEM((3, SEG, D), BF16),
            pltpu.SemaphoreType.DMA((3,)),
            heads(NHEAD, BF16), heads(NHEAD, BF16), heads(NHEAD, BF16), heads(NHEAD, BF16),
            pltpu.VMEM((NHEAD, SEG, SEG), F32),
            pltpu.VMEM((NHEAD, SEG, SEG), BF16),
            heads(NHEAD, F32),
            pltpu.VMEM((NHEAD, 8, SEG), F32),
            pltpu.VMEM((D, SEG), BF16),
            heads(NHEAD, F32), heads(NHEAD, F32), heads(NHEAD, F32),
            heads(2, BF16), heads(2, BF16), heads(2, BF16), heads(2, BF16),
            pltpu.VMEM((2, SEG, SEG), BF16),
            heads(2, F32),
            pltpu.VMEM((2, 8, SEG), F32),
            pltpu.VMEM((3, PAIR, SEG), F32),
            pltpu.VMEM((SPREAD, PACK3, 128), BF16), pltpu.VMEM((SPREAD, PACK3, 128), BF16),
            pltpu.VMEM((SPREAD, PACK1, 128), BF16), pltpu.VMEM((SPREAD, PACK1, 128), BF16),
            pltpu.VMEM((SPREAD, 8, 128), F32), pltpu.VMEM((SPREAD, 8, 128), F32),
            pltpu.VMEM((SPREAD // 2, 2, PACK1, 128), BF16),
            pltpu.VMEM((SPREAD, 2, PACK1, 128), BF16),
            pltpu.VMEM((SPREAD, 8, 128), F32), pltpu.VMEM((SPREAD, 8, 128), F32),
            pltpu.VMEM((SPREAD, PACK3, 128), BF16), pltpu.VMEM((SPREAD, PACK3, 128), BF16),
            pltpu.SemaphoreType.DMA((6, SPREAD)),
            pltpu.SemaphoreType.DMA((6, SPREAD)),
            pltpu.VMEM((NZ * z_pad, 128), BF16), pltpu.VMEM((NZ * z_pad, 128), BF16),
            pltpu.VMEM((D, SEG), BF16),
            pltpu.VMEM((D, SEG), BF16),
            pltpu.VMEM((NHEAD, SEG), F32), pltpu.VMEM((NHEAD, SEG), F32),
            pltpu.VMEM((COLH, SEG), BF16),
            pltpu.VMEM((NY * NX, DROWS, 128), BF16), pltpu.VMEM((NY * NX, DROWS, 128), BF16),
            pltpu.VMEM((NZ, z_pad, 128), BF16), pltpu.VMEM((NZ, z_pad, 128), BF16),
            pltpu.SemaphoreType.DMA((2, 3)),
            pltpu.SemaphoreType.DMA((2, NY * NX)),
            pltpu.SemaphoreType.DMA((2, NZ)),
        ],
        compiler_params=pltpu.CompilerParams(
            collective_id=0, has_side_effects=True, vmem_limit_bytes=VMEM_LIMIT
        ),
    )(queries, keys, values, out_grad, out_weight, slide_lengths)
    out = jax.ShapeDtypeStruct((SEG, D), BF16)
    return pl.pallas_call(
        final_kernel,
        out_shape=(out, out, out, jax.ShapeDtypeStruct((z_rows, COLS), F32)),
        in_specs=[pl.BlockSpec(memory_space=pl.ANY), vmem],
        out_specs=(pl.BlockSpec(memory_space=pl.ANY),) * 3 + (vmem,),
        scratch_shapes=[
            pltpu.VMEM((3, SEG, D), BF16),
            pltpu.SemaphoreType.DMA((3,)),
            pltpu.SemaphoreType.DMA((3,)),
        ],
        compiler_params=pltpu.CompilerParams(vmem_limit_bytes=VMEM_LIMIT),
    )(grads, partial)


def solution(mesh):
    placed = (
        P(("dp", "seq"), None),
        P(("dp", "seq"), None),
        P(("dp", "seq"), None),
        P(("dp", "seq"), None),
        P(),
        P("dp", None),
    )
    return jax.shard_map(
        on_device,
        mesh=mesh,
        in_specs=placed,
        out_specs=(
            P(("dp", "seq"), None),
            P(("dp", "seq"), None),
            P(("dp", "seq"), None),
            P("dp", "seq"),
        ),
        check_vma=False,
    )
```

```python
import functools

import jax
import jax.numpy as jnp
from jax import lax
from jax.experimental import pallas as pl
from jax.experimental.pallas import tpu as pltpu
from jax.sharding import PartitionSpec as P

MESH = pl.DeviceIdType.MESH
NHEAD = 16
DH = 48
D = NHEAD * DH
SEG = 256
SPREAD = 8
CLS = SEG // SPREAD
PAIR = 2 * DH
DENSE = PAIR // 4
PACK1 = 32
PACK3 = 80
SLIDES = 4
NX = 4
UF = 8
UB = 8
NY = 4
NZ = 16
COLS = D // SPREAD
COLH = D // 2
MAIN = 128
REM = D // NY - MAIN
DROWS = COLS + COLS // 2
PAD = 16
BIG = 2.0**20
VMEM_LIMIT = 60 * 1024 * 1024
LOG2E = 1.4426950408889634
SCALE = DH**-0.5
F32 = jnp.float32
BF16 = jnp.bfloat16


def iota(shape, dim):
    return lax.broadcasted_iota(jnp.int32, shape, dim)


def mm(a, b):
    return jnp.dot(a, b, preferred_element_type=F32)


def mm_tn(a, b):
    return lax.dot_general(a, b, (((0,), (0,)), ((), ())), preferred_element_type=F32)


def mm_nt(a, b):
    return lax.dot_general(a, b, (((1,), (1,)), ((), ())), preferred_element_type=F32)


def mask_rows(pos, ends):
    row = iota((PAD, pos.shape[1]), 0)
    starts = [0] + ends[:-1]
    hit = jnp.zeros((PAD, pos.shape[1]), F32)
    for i in range(SLIDES):
        inside = jnp.where((pos >= starts[i]) & (pos < ends[i]), 1.0, 0.0)
        hit = jnp.where(row == i, inside, hit)
    off = jnp.where(row < SLIDES, (hit - 1.0) * BIG, 0.0)
    return hit.astype(BF16), off.astype(BF16)


def scores(qt, kt, k_mask, q_mask):
    return mm_tn(jnp.concatenate([kt, k_mask], 0), jnp.concatenate([qt, q_mask], 0))


def weigh(s, top, vt, ones):
    top = top * (SCALE * LOG2E)
    e = jnp.exp2(s * (SCALE * LOG2E) - top).astype(BF16)
    ov = mm(jnp.concatenate([vt, ones], 0), e)
    total = ov[DH : DH + 1]
    return e, ov[:DH] * (1.0 / total), top, top + jnp.log(total) * LOG2E


def forward_head(qt, kt, vt, k_mask, q_mask, ones):
    s = scores(qt, kt, k_mask, q_mask)
    return weigh(s, jnp.max(s, 0, keepdims=True), vt, ones)


def backward_head(qt, kt, vt, dot, e, ones, ratio, delta):
    hi = delta.astype(BF16)
    lo = (delta - hi.astype(F32)).astype(BF16)
    row = iota((PAD, delta.shape[1]), 0)
    less = jnp.where(row == 0, -hi.astype(F32), jnp.where(row == 1, -lo.astype(F32), 0.0))
    dp = mm_tn(jnp.concatenate([vt, ones], 0), jnp.concatenate([dot, less.astype(BF16)], 0))
    g = (e.astype(F32) * dp).astype(BF16)
    dv = mm_nt((dot.astype(F32) * ratio).astype(BF16), e)
    ratio = ratio * SCALE
    dk = mm_nt((qt.astype(F32) * ratio).astype(BF16), g)
    dq = mm(kt, g) * ratio
    return dq, dk, dv


def blend(lse_a, lse_b):
    top = jnp.maximum(lse_a, lse_b)
    lse = top + jnp.log(jnp.exp2(lse_a - top) + jnp.exp2(lse_b - top)) * LOG2E
    return lse, jnp.exp2(lse_a - lse), jnp.exp2(lse_b - lse)


def three_terms(x):
    out = []
    for _ in range(3):
        out.append(x.astype(BF16).astype(F32))
        x = x - out[-1]
    return jnp.concatenate(out + [jnp.zeros((5, x.shape[1]), F32)], 0)


def lane_block(rows):
    return iota((rows, 128), 1) // CLS


def up(n, to):
    return (n + to - 1) // to * to


def far_first(size):
    return sorted(range(1, size), key=lambda d: -min(d, size - d))


def shift(x, blocks):
    blocks = blocks % 4
    return x if blocks == 0 else pltpu.roll(x, blocks * CLS, 1)


def pack(parts, j, rows):
    out = []
    block = lane_block(DENSE)
    for x in parts:
        dense = jnp.zeros((DENSE, 128), F32)
        for b in range(4):
            dense = jnp.where(block == b, shift(x[b * DENSE : (b + 1) * DENSE], b - j), dense)
        out.append(dense)
    if rows > len(parts) * DENSE:
        out.append(jnp.zeros((rows - len(parts) * DENSE, 128), F32))
    return jnp.concatenate(out, 0)


def unpack(x, t, j):
    x = x[t * DENSE : (t + 1) * DENSE]
    return jnp.concatenate([shift(x, j - b) for b in range(4)], 0)


def kernel(
    q_in, k_in, v_in, g_in, w_in, len_in,
    grads_ref, dw_ref,
    q_ref, k_ref, v_ref, g_ref, w_ref, len_ref, isem, grads, osem,
    qt, kt, vt, dot, s_all, e_all, ot, sta, att, dqt, dkt, dvt,
    qb, kb, vb, db, eb, ob, sb,
    gb, send0, recv0, send1, recv1, send2, recv2, send3, recv3, send4, recv4, send5, recv5,
    ssem, rsem, pick_main, pick_rest,
    ogt, att_x, lse_own, lse_x, og_x,
    d_send, d_recv, z_send, z_recv, c_sem, d_sem, z_sem,
):
    dp = lax.axis_index("dp")
    me = lax.axis_index("seq")
    my, mz, mx, mc = dp // NZ, dp % NZ, me // 2, me % 2
    z_rows = D // (NY * NZ)
    z_pad = up(z_rows, 16)

    loads = []
    for i, (src, dst) in enumerate(
        (
            (q_in, q_ref), (k_in, k_ref), (v_in, v_ref), (g_in, g_ref), (w_in, w_ref),
            (len_in, len_ref),
        )
    ):
        loads.append(pltpu.make_async_copy(src, dst, isem.at[i]))
    for c in loads[:3]:
        c.start()

    barrier = pltpu.get_barrier_semaphore()
    for d in far_first(NZ):
        pl.semaphore_signal(
            barrier, inc=1, device_id=(my * NZ + lax.rem(mz + d, NZ), me), device_id_type=MESH
        )
    for d in range(1, NY):
        for x in range(NX):
            other = (lax.rem(my + d, NY) * NZ + mz, 2 * x + me // 4)
            pl.semaphore_signal(barrier, inc=1, device_id=other, device_id_type=MESH)
    for d in range(1, SPREAD):
        pl.semaphore_signal(
            barrier, inc=1, device_id=(dp, lax.rem(me + d, SPREAD)), device_id_type=MESH
        )

    def exchange(kind, send, recv, group=1):
        copies = []
        for d in far_first(SPREAD):
            other = lax.rem(me + d, SPREAD)
            copies.append(
                pltpu.make_async_remote_copy(
                    src_ref=send.at[other // group],
                    dst_ref=recv.at[me],
                    send_sem=ssem.at[kind, d],
                    recv_sem=rsem.at[kind, d],
                    device_id=(dp, other),
                    device_id_type=MESH,
                )
            )
            copies[-1].start()
        return copies

    def arrive(kind, send, recv, group=1):
        for d in range(1, SPREAD):
            source = lax.rem(me + SPREAD - d, SPREAD)
            pltpu.make_async_remote_copy(
                src_ref=send.at[source // group],
                dst_ref=recv.at[source],
                send_sem=ssem.at[kind, d],
                recv_sem=rsem.at[kind, d],
                device_id=(dp, source),
                device_id_type=MESH,
            ).wait_recv()

    def along(size, place, device, send, recv, sem):
        def copy(d, slot, other):
            return pltpu.make_async_remote_copy(
                src_ref=send.at[other],
                dst_ref=recv.at[slot],
                send_sem=sem.at[0, d],
                recv_sem=sem.at[1, d],
                device_id=device(other),
                device_id_type=MESH,
            )

        def start():
            for d in far_first(size):
                copy(d, place, lax.rem(place + d, size)).start()
            recv[place] = send[place]

        def finish():
            for d in range(1, size):
                source = lax.rem(place + size - d, size)
                copy(d, source, source).wait_recv()

        def sent():
            for d in range(1, size):
                copy(d, place, lax.rem(place + d, size)).wait_send()

        return start, finish, sent

    def plane_each(do, own=None):
        for d in (2, 1, 3, 0):
            y = lax.rem(my + d, NY)
            for b in range(NX):
                other = 4 * mc + b
                copy = pltpu.make_async_remote_copy(
                    src_ref=d_send.at[y * NX + b],
                    dst_ref=d_recv.at[d * NX + mx],
                    send_sem=d_sem.at[0, d * NX + b],
                    recv_sem=d_sem.at[1, d * NX + mx],
                    device_id=(y * NZ + mz, other),
                    device_id_type=MESH,
                )
                if d:
                    do(copy)
                else:
                    pl.when(other != me)(functools.partial(do, copy))
                    if own is not None:
                        pl.when(other == me)(functools.partial(own, b))

    def plane_own(b):
        d_recv[mx] = d_send[my * NX + b]

    def plane_arrive():
        for d in (0, 1, 3, 2):
            y = lax.rem(my + NY - d, NY)
            for x in range(NX):
                source = 2 * x + me // 4
                copy = pltpu.make_async_remote_copy(
                    src_ref=d_send.at[0],
                    dst_ref=d_recv.at[d * NX + x],
                    send_sem=d_sem.at[0, d * NX],
                    recv_sem=d_sem.at[1, d * NX + x],
                    device_id=(y * NZ + mz, source),
                    device_id_type=MESH,
                )
                if d:
                    copy.wait_recv()
                else:
                    pl.when(source != me)(copy.wait_recv)

    def total(recv, count):
        out = recv[0].astype(F32)
        for i in range(1, count):
            out = out + recv[i].astype(F32)
        return out

    to = iota((SEG, SEG), 1)
    at = iota((SEG, SEG), 0)
    perm = jnp.where(at == to % CLS * SPREAD + to // CLS, 1.0, 0.0).astype(BF16)
    for i, (src, dst) in enumerate(((q_ref, qt), (k_ref, kt), (v_ref, vt))):
        loads[i].wait()
        if i == 0:
            for c in loads[3:]:
                c.start()
        dst[...] = mm_tn(src[...], perm).astype(BF16).reshape(NHEAD, DH, SEG)
    def class_rows(src, j):
        tile = pl.ds(j // 4 * 128, 128)
        both = jnp.concatenate([src[j, :, tile], src[j + SPREAD, :, tile]], 0)
        return both.astype(F32)

    for j in range(SPREAD):
        send0[j] = pack([class_rows(x, j) for x in (qt, kt, vt)], j, PACK3).astype(BF16)
    recv0[me] = send0[me]
    pl.semaphore_wait(barrier, SPREAD - 1 + (NY - 1) * NX + NZ - 1)
    copies = exchange(0, send0, recv0)

    loads[3].wait()
    ogt[...] = mm_tn(g_ref[...], perm).astype(BF16)
    loads[4].wait()
    dot[...] = mm(w_ref[...], ogt[...]).astype(BF16).reshape(NHEAD, DH, SEG)
    for j in range(SPREAD):
        send1[j] = pack([class_rows(dot, j)], j, PACK1).astype(BF16)
    recv1[me] = send1[me]
    copies += exchange(1, send1, recv1)
    z_at = iota((NZ * z_pad, 128), 0)
    lane = iota((NZ * z_pad, 128), 1)
    z_at = jnp.where(z_at % z_pad < z_rows, z_at // z_pad * z_rows + z_at % z_pad, -1)
    pick_main[...] = jnp.where(lane == z_at, 1.0, 0.0).astype(BF16)
    pick_rest[...] = jnp.where(lane + MAIN == z_at, 1.0, 0.0).astype(BF16)

    loads[5].wait()
    ends = []
    for i in range(SLIDES):
        ends.append(len_ref[0, i] if i == 0 else ends[-1] + len_ref[0, i])
    lane = iota((1, SEG), 1)
    k_mask, q_mask = mask_rows(me * SEG + lane % CLS * SPREAD + lane // CLS, ends)
    row = iota((PAD, SEG), 0)
    ones = jnp.where(row < 2, 1.0, 0.0).astype(BF16)

    def forward_s(h):
        s = scores(qt[h], kt[h], k_mask, q_mask)
        s_all[h] = s
        sta[h, 0:1] = jnp.max(s, 0, keepdims=True)

    def forward_o(h):
        e, o, top, lse = weigh(s_all[h], sta[h, 0:1], vt[h], ones)
        e_all[h] = e
        ot[h] = o
        att[pl.ds(pl.multiple_of(h * DH, 16), DH)] = o.astype(BF16)
        sta[h, 0:1] = top
        sta[h, 1:2] = lse
        sta[h, 2:3] = jnp.sum(dot[h].astype(F32) * o, 0, keepdims=True)

    def loop(body, first, last, unroll):
        def step(i, carry):
            for u in range(unroll):
                body(i * unroll + u)
            return carry

        lax.fori_loop(first // unroll, last // unroll, step, 0)

    loop(forward_s, 0, NHEAD, UF)
    loop(forward_o, 0, NHEAD, UF)

    lse_own[...] = sta[:, 1, :]
    early = [
        (att, att_x),
        (lse_own, lse_x),
        (ogt.at[pl.ds(pl.multiple_of((1 - mc) * COLH, 128), COLH)], og_x),
    ]
    sibling = [
        pltpu.make_async_remote_copy(
            src_ref=src,
            dst_ref=dst,
            send_sem=c_sem.at[0, i],
            recv_sem=c_sem.at[1, i],
            device_id=(dp, 2 * mx + 1 - mc),
            device_id_type=MESH,
        )
        for i, (src, dst) in enumerate(early)
    ]
    for c in sibling:
        c.start()

    narrow = lane_block(8)
    for j in range(SPREAD):
        tile = pl.ds(j // 4 * 128, 128)
        rows = jnp.concatenate(
            [sta[j, 1:2, tile], sta[j + SPREAD, 1:2, tile],
             sta[j, 2:3, tile], sta[j + SPREAD, 2:3, tile],
             jnp.zeros((4, 128), F32)], 0)
        send2[j] = shift(rows, -j)
    recv2[me] = send2[me]
    copies += exchange(2, send2, recv2)

    block = lane_block(PAIR)

    def gather(recv, dsts):
        for half in range(2):
            tile = pl.ds(half * 128, 128)
            outs = [jnp.zeros((PAIR, 128), F32)] * len(dsts)
            for s in range(half * 4, half * 4 + 4):
                got = recv[s].astype(F32)
                for t in range(len(dsts)):
                    outs[t] = jnp.where(block == s % 4, unpack(got, t, s), outs[t])
            for dst, out in zip(dsts, outs):
                out = out.astype(BF16)
                for u in range(2):
                    dst[u, :, tile] = out[u * DH : (u + 1) * DH]

    arrive(0, send0, recv0)
    gather(recv0, (qb, kb, vb))
    kb_mask, qb_mask = mask_rows(lane * SPREAD + me, ends)
    for u in range(2):
        e, o, top, lse = forward_head(qb[u], kb[u], vb[u], kb_mask, qb_mask, ones)
        eb[u] = e
        ob[u] = o
        sb[u, 0:1] = top
        sb[u, 1:2] = lse
    for s in range(SPREAD):
        tile = pl.ds(s // 4 * 128, 128)
        both = jnp.concatenate([ob[0, :, tile], ob[1, :, tile]], 0)
        lses = jnp.where(
            lane_block(1) == 0, shift(sb[0, 1:2, tile], -s), shift(sb[1, 1:2, tile], 1 - s)
        )
        dense = jnp.concatenate([pack([both], s, DENSE), three_terms(lses)], 0)
        send3[s // 2, s % 2] = dense.astype(BF16)
    recv3[me] = send3[mx]
    copies += exchange(3, send3, recv3, 2)
    arrive(1, send1, recv1)
    gather(recv1, (db,))
    for u in range(2):
        sb[u, 2:3] = jnp.sum(db[u].astype(F32) * ob[u], 0, keepdims=True)
    for s in range(SPREAD):
        tile = pl.ds(s // 4 * 128, 128)
        rows = jnp.concatenate([sb[0, 2:3, tile], sb[1, 2:3, tile], jnp.zeros((6, 128), F32)], 0)
        send4[s] = shift(rows, -s)
    recv4[me] = send4[me]
    copies += exchange(4, send4, recv4)

    tall = iota((NHEAD, 128), 0)
    spot = lane_block(NHEAD)

    def spread_rows(pairs, empty):
        sides = []
        for half in range(2):
            out = jnp.full((NHEAD, 128), empty, F32)
            for j in range(half * 4, half * 4 + 4):
                for u in range(2):
                    here = (tall == j + SPREAD * u) & (spot == j % 4)
                    out = jnp.where(here, pairs[j][u], out)
            sides.append(out)
        return jnp.concatenate(sides, 1)

    def combine(which, lse_a, target):
        got = [recv3[j, which].astype(F32) for j in range(SPREAD)]
        pairs = []
        for j in range(SPREAD):
            x = got[j][DENSE : DENSE + 1] + got[j][DENSE + 1 : DENSE + 2]
            x = x + got[j][DENSE + 2 : DENSE + 3]
            pairs.append((shift(x, j), shift(x, j - 1)))
        lse, w_a, w_b = blend(lse_a, spread_rows(pairs, -1e30))
        for j in range(SPREAD):
            other = unpack(got[j], 0, j)
            tile = slice(j // 4 * 128, j // 4 * 128 + 128)
            for u in range(2):
                h = j + SPREAD * u
                mine = target[h * DH : (h + 1) * DH, tile].astype(F32)
                both = mine * w_a[h : h + 1, tile]
                both = both + other[u * DH : (u + 1) * DH] * w_b[h : h + 1, tile]
                x = jnp.where(lane_block(DH) == j % 4, both, mine)
                target[h * DH : (h + 1) * DH, tile] = x.astype(BF16)
        return lse, w_a, w_b

    for c in sibling:
        c.wait()
    arrive(3, send3, recv3, 2)
    lse, w_a, w_b = combine(mc, lse_own[...], att)
    combine(1 - mc, lse_x[...], att_x)

    def part(first, count):
        out = 0.0
        for rows, cols in (
            (att, ogt.at[pl.ds(pl.multiple_of(mc * COLH, 128), COLH)]),
            (att_x, og_x),
        ):
            starts = [y * (MAIN + REM) + first for y in range(NY)]
            x = jnp.concatenate([rows[i : i + count] for i in starts], 0)
            out = out + mm_nt(cols[...], x)
        return out

    zz = along(NZ, mz, lambda z: (my * NZ + z, me), z_send, z_recv, z_sem)
    main, rest = part(0, MAIN), part(MAIN, REM)
    low = iota((COLS // 2, 128), 1) < REM
    for y in range(NY):
        for b in range(NX):
            d_send[y * NX + b, :COLS] = main[
                b * COLS : (b + 1) * COLS, y * MAIN : (y + 1) * MAIN
            ].astype(BF16)
            x = rest[b * COLS : (b + 1) * COLS, y // 2 * 128 : y // 2 * 128 + 128]
            top, bottom = x[: COLS // 2], x[COLS // 2 :]
            if y % 2:
                top = pltpu.roll(top, REM, 1)
            else:
                bottom = pltpu.roll(bottom, REM, 1)
            d_send[y * NX + b, COLS:] = jnp.where(low, top, bottom).astype(BF16)
    plane_each(lambda copy: copy.start(), plane_own)

    arrive(4, send4, recv4)
    pairs = []
    for j in range(SPREAD):
        x = shift(recv4[j], j)
        pairs.append((x[0:1], x[1:2]))
    sta[:, 2, :] = w_a * sta[:, 2, :] + w_b * spread_rows(pairs, 0.0)
    sta[:, 3, :] = jnp.exp2(sta[:, 0, :] - lse)

    def step_z():
        plane_arrive()
        x = total(d_recv, NY * NX)
        rest = jnp.concatenate([x[COLS:], pltpu.roll(x[COLS:], REM, 1)], 0)
        pad = jnp.zeros((128 - COLS, 128), F32)
        x = jnp.concatenate([x[:COLS], pad], 0).astype(BF16)
        rest = jnp.concatenate([rest, pad], 0).astype(BF16)
        x = (mm_nt(pick_main[...], x) + mm_nt(pick_rest[...], rest)).astype(BF16)
        for z in range(NZ):
            z_send[z] = x[z * z_pad : (z + 1) * z_pad]
        zz[0]()

    def finish():
        zz[1]()
        dw_ref[...] = total(z_recv, NZ)

    arrive(2, send2, recv2)
    halves = []
    for half in range(2):
        out = jnp.zeros((8, 128), F32)
        for s in range(half * 4, half * 4 + 4):
            out = jnp.where(narrow == s % 4, shift(recv2[s], s), out)
        halves.append(out)
    theirs = jnp.concatenate(halves, 1)
    for u in range(2):
        top = sb[u, 0:1]
        lse, w_a, w_b = blend(theirs[u : u + 1], sb[u, 1:2])
        delta = w_a * theirs[2 + u : 3 + u] + w_b * sb[u, 2:3]
        grads_b = backward_head(
            qb[u], kb[u], vb[u], db[u], eb[u], ones, jnp.exp2(top - lse), delta
        )
        for t in range(3):
            gb[t, u * DH : (u + 1) * DH] = grads_b[t]
    for s in range(SPREAD):
        tile = pl.ds(s // 4 * 128, 128)
        send5[s] = pack([gb[t, :, tile] for t in range(3)], s, PACK3).astype(BF16)
    recv5[me] = send5[me]

    def backward(h):
        dq, dk, dv = backward_head(
            qt[h], kt[h], vt[h], dot[h], e_all[h], ones, sta[h, 3:4], sta[h, 2:3]
        )
        dqt[h] = dq
        dkt[h] = dk
        dvt[h] = dv

    copies += exchange(5, send5, recv5)
    loop(backward, 0, NHEAD, UB)
    step_z()

    arrive(5, send5, recv5)
    for j in range(SPREAD):
        tile = pl.ds(j // 4 * 128, 128)
        got = recv5[j].astype(F32)
        for t, dst in enumerate((dqt, dkt, dvt)):
            part = jnp.where(block == j % 4, unpack(got, t, j), 0.0)
            for u in range(2):
                h = j + SPREAD * u
                dst[h, :, tile] = dst[h, :, tile] + part[u * DH : (u + 1) * DH]
    stores = []
    for t, src in enumerate((dqt, dkt, dvt)):
        grads[t] = mm_nt(perm, src[...].reshape(D, SEG).astype(BF16)).astype(BF16)
        stores.append(pltpu.make_async_copy(grads.at[t], grads_ref.at[t], osem.at[t]))
        stores[-1].start()

    finish()
    for c in stores:
        c.wait()
    for c in copies:
        c.wait_send()
    plane_each(lambda copy: copy.wait_send())
    zz[2]()


def final_kernel(grads_ref, part_ref, dq_ref, dk_ref, dv_ref, dw_ref, x, part, dw, isem, osem):
    loads = [pltpu.make_async_copy(grads_ref.at[t], x.at[t], isem.at[t]) for t in range(3)]
    loads.append(pltpu.make_async_copy(part_ref, part, isem.at[3]))
    for c in loads:
        c.start()
    stores = []
    for t, dst in enumerate((dq_ref, dk_ref, dv_ref)):
        loads[t].wait()
        stores.append(pltpu.make_async_copy(x.at[t], dst, osem.at[t]))
        stores[-1].start()
    loads[3].wait()
    dw[...] = part[0 : dw.shape[0], 0 : dw.shape[1]]
    stores.append(pltpu.make_async_copy(dw, dw_ref, osem.at[3]))
    stores[-1].start()
    for c in stores:
        c.wait()


def on_device(queries, keys, values, out_grad, out_weight, slide_lengths):
    vmem = pl.BlockSpec(memory_space=pltpu.VMEM)
    heads = lambda n, dtype: pltpu.VMEM((n, DH, SEG), dtype)
    z_rows = D // (NY * NZ)
    z_pad = up(z_rows, 16)
    grads, partial = pl.pallas_call(
        kernel,
        out_shape=(
            jax.ShapeDtypeStruct((3, SEG, D), BF16),
            jax.ShapeDtypeStruct((z_pad, 128), F32),
        ),
        in_specs=[pl.BlockSpec(memory_space=pl.ANY)] * 6,
        out_specs=(pl.BlockSpec(memory_space=pl.ANY), vmem),
        scratch_shapes=[
            pltpu.VMEM((SEG, D), BF16), pltpu.VMEM((SEG, D), BF16), pltpu.VMEM((SEG, D), BF16),
            pltpu.VMEM((SEG, D), BF16), pltpu.VMEM((D, D), BF16),
            pltpu.SMEM((1, SLIDES), jnp.int32),
            pltpu.SemaphoreType.DMA((6,)),
            pltpu.VMEM((3, SEG, D), BF16),
            pltpu.SemaphoreType.DMA((3,)),
            heads(NHEAD, BF16), heads(NHEAD, BF16), heads(NHEAD, BF16), heads(NHEAD, BF16),
            pltpu.VMEM((NHEAD, SEG, SEG), F32),
            pltpu.VMEM((NHEAD, SEG, SEG), BF16),
            heads(NHEAD, F32),
            pltpu.VMEM((NHEAD, 8, SEG), F32),
            pltpu.VMEM((D, SEG), BF16),
            heads(NHEAD, F32), heads(NHEAD, F32), heads(NHEAD, F32),
            heads(2, BF16), heads(2, BF16), heads(2, BF16), heads(2, BF16),
            pltpu.VMEM((2, SEG, SEG), BF16),
            heads(2, F32),
            pltpu.VMEM((2, 8, SEG), F32),
            pltpu.VMEM((3, PAIR, SEG), F32),
            pltpu.VMEM((SPREAD, PACK3, 128), BF16), pltpu.VMEM((SPREAD, PACK3, 128), BF16),
            pltpu.VMEM((SPREAD, PACK1, 128), BF16), pltpu.VMEM((SPREAD, PACK1, 128), BF16),
            pltpu.VMEM((SPREAD, 8, 128), F32), pltpu.VMEM((SPREAD, 8, 128), F32),
            pltpu.VMEM((SPREAD // 2, 2, PACK1, 128), BF16),
            pltpu.VMEM((SPREAD, 2, PACK1, 128), BF16),
            pltpu.VMEM((SPREAD, 8, 128), F32), pltpu.VMEM((SPREAD, 8, 128), F32),
            pltpu.VMEM((SPREAD, PACK3, 128), BF16), pltpu.VMEM((SPREAD, PACK3, 128), BF16),
            pltpu.SemaphoreType.DMA((6, SPREAD)),
            pltpu.SemaphoreType.DMA((6, SPREAD)),
            pltpu.VMEM((NZ * z_pad, 128), BF16), pltpu.VMEM((NZ * z_pad, 128), BF16),
            pltpu.VMEM((D, SEG), BF16),
            pltpu.VMEM((D, SEG), BF16),
            pltpu.VMEM((NHEAD, SEG), F32), pltpu.VMEM((NHEAD, SEG), F32),
            pltpu.VMEM((COLH, SEG), BF16),
            pltpu.VMEM((NY * NX, DROWS, 128), BF16), pltpu.VMEM((NY * NX, DROWS, 128), BF16),
            pltpu.VMEM((NZ, z_pad, 128), BF16), pltpu.VMEM((NZ, z_pad, 128), BF16),
            pltpu.SemaphoreType.DMA((2, 3)),
            pltpu.SemaphoreType.DMA((2, NY * NX)),
            pltpu.SemaphoreType.DMA((2, NZ)),
        ],
        compiler_params=pltpu.CompilerParams(
            collective_id=0, has_side_effects=True, vmem_limit_bytes=VMEM_LIMIT
        ),
    )(queries, keys, values, out_grad, out_weight, slide_lengths)
    out = jax.ShapeDtypeStruct((SEG, D), BF16)
    return pl.pallas_call(
        final_kernel,
        out_shape=(out, out, out, jax.ShapeDtypeStruct((z_rows, COLS), F32)),
        in_specs=[pl.BlockSpec(memory_space=pl.ANY)] * 2,
        out_specs=(pl.BlockSpec(memory_space=pl.ANY),) * 4,
        scratch_shapes=[
            pltpu.VMEM((3, SEG, D), BF16),
            pltpu.VMEM((z_pad, 128), F32),
            pltpu.VMEM((z_rows, COLS), F32),
            pltpu.SemaphoreType.DMA((4,)),
            pltpu.SemaphoreType.DMA((4,)),
        ],
        compiler_params=pltpu.CompilerParams(vmem_limit_bytes=VMEM_LIMIT),
    )(grads, partial)


def solution(mesh):
    placed = (
        P(("dp", "seq"), None),
        P(("dp", "seq"), None),
        P(("dp", "seq"), None),
        P(("dp", "seq"), None),
        P(),
        P("dp", None),
    )
    return jax.shard_map(
        on_device,
        mesh=mesh,
        in_specs=placed,
        out_specs=(
            P(("dp", "seq"), None),
            P(("dp", "seq"), None),
            P(("dp", "seq"), None),
            P("dp", "seq"),
        ),
        check_vma=False,
    )
```

```python
import functools

import jax
import jax.numpy as jnp
from jax import lax
from jax.experimental import pallas as pl
from jax.experimental.pallas import tpu as pltpu
from jax.sharding import PartitionSpec as P

MESH = pl.DeviceIdType.MESH
NHEAD = 16
DH = 48
D = NHEAD * DH
SEG = 256
SPREAD = 8
CLS = SEG // SPREAD
PAIR = 2 * DH
DENSE = PAIR // 4
PACK1 = 32
PACK3 = 80
SLIDES = 4
NX = 4
UF = 8
UB = 8
NY = 4
NZ = 16
COLS = D // SPREAD
COLH = D // 2
MAIN = 128
REM = D // NY - MAIN
DROWS = COLS + COLS // 2
PAD = 16
BIG = 2.0**20
VMEM_LIMIT = 60 * 1024 * 1024
LOG2E = 1.4426950408889634
SCALE = DH**-0.5
F32 = jnp.float32
BF16 = jnp.bfloat16


def iota(shape, dim):
    return lax.broadcasted_iota(jnp.int32, shape, dim)


def mm(a, b):
    return jnp.dot(a, b, preferred_element_type=F32)


def mm_tn(a, b):
    return lax.dot_general(a, b, (((0,), (0,)), ((), ())), preferred_element_type=F32)


def mm_nt(a, b):
    return lax.dot_general(a, b, (((1,), (1,)), ((), ())), preferred_element_type=F32)


def mask_rows(pos, ends):
    row = iota((PAD, pos.shape[1]), 0)
    starts = [0] + ends[:-1]
    hit = jnp.zeros((PAD, pos.shape[1]), F32)
    for i in range(SLIDES):
        inside = jnp.where((pos >= starts[i]) & (pos < ends[i]), 1.0, 0.0)
        hit = jnp.where(row == i, inside, hit)
    off = jnp.where(row < SLIDES, (hit - 1.0) * BIG, 0.0)
    return hit.astype(BF16), off.astype(BF16)


def scores(qt, kt, k_mask, q_mask):
    return mm_tn(jnp.concatenate([kt, k_mask], 0), jnp.concatenate([qt, q_mask], 0))


def weigh(s, top, vt, ones):
    top = top * (SCALE * LOG2E)
    e = jnp.exp2(s * (SCALE * LOG2E) - top).astype(BF16)
    ov = mm(jnp.concatenate([vt, ones], 0), e)
    total = ov[DH : DH + 1]
    return e, ov[:DH] * (1.0 / total), top, top + jnp.log(total) * LOG2E


def forward_head(qt, kt, vt, k_mask, q_mask, ones):
    s = scores(qt, kt, k_mask, q_mask)
    return weigh(s, jnp.max(s, 0, keepdims=True), vt, ones)


def backward_head(qt, kt, vt, dot, e, ones, ratio, delta):
    hi = delta.astype(BF16)
    lo = (delta - hi.astype(F32)).astype(BF16)
    row = iota((PAD, delta.shape[1]), 0)
    less = jnp.where(row == 0, -hi.astype(F32), jnp.where(row == 1, -lo.astype(F32), 0.0))
    dp = mm_tn(jnp.concatenate([vt, ones], 0), jnp.concatenate([dot, less.astype(BF16)], 0))
    g = (e.astype(F32) * dp).astype(BF16)
    dv = mm_nt((dot.astype(F32) * ratio).astype(BF16), e)
    ratio = ratio * SCALE
    dk = mm_nt((qt.astype(F32) * ratio).astype(BF16), g)
    dq = mm(kt, g) * ratio
    return dq, dk, dv


def blend(lse_a, lse_b):
    top = jnp.maximum(lse_a, lse_b)
    lse = top + jnp.log(jnp.exp2(lse_a - top) + jnp.exp2(lse_b - top)) * LOG2E
    return lse, jnp.exp2(lse_a - lse), jnp.exp2(lse_b - lse)


def three_terms(x):
    out = []
    for _ in range(3):
        out.append(x.astype(BF16).astype(F32))
        x = x - out[-1]
    return jnp.concatenate(out + [jnp.zeros((5, x.shape[1]), F32)], 0)


def lane_block(rows):
    return iota((rows, 128), 1) // CLS


def up(n, to):
    return (n + to - 1) // to * to


def far_first(size):
    return sorted(range(1, size), key=lambda d: -min(d, size - d))


def shift(x, blocks):
    blocks = blocks % 4
    return x if blocks == 0 else pltpu.roll(x, blocks * CLS, 1)


def pack(parts, j, rows):
    out = []
    block = lane_block(DENSE)
    for x in parts:
        dense = jnp.zeros((DENSE, 128), F32)
        for b in range(4):
            dense = jnp.where(block == b, shift(x[b * DENSE : (b + 1) * DENSE], b - j), dense)
        out.append(dense)
    if rows > len(parts) * DENSE:
        out.append(jnp.zeros((rows - len(parts) * DENSE, 128), F32))
    return jnp.concatenate(out, 0)


def unpack(x, t, j):
    x = x[t * DENSE : (t + 1) * DENSE]
    return jnp.concatenate([shift(x, j - b) for b in range(4)], 0)


def kernel(
    q_in, k_in, v_in, g_in, w_in, len_in,
    grads_ref, dw_ref,
    q_ref, k_ref, v_ref, g_ref, w_ref, len_ref, isem, grads, osem,
    qt, kt, vt, dot, s_all, e_all, ot, sta, att, dqt, dkt, dvt,
    qb, kb, vb, db, eb, ob, sb,
    gb, send0, recv0, send1, recv1, send2, recv2, send3, recv3, send4, recv4, send5, recv5,
    ssem, rsem, pick_main, pick_rest,
    ogt, att_x, lse_own, lse_x, og_x,
    d_send, d_recv, z_send, z_recv, c_sem, d_sem, z_sem,
):
    dp = lax.axis_index("dp")
    me = lax.axis_index("seq")
    my, mz, mx, mc = dp // NZ, dp % NZ, me // 2, me % 2
    z_rows = D // (NY * NZ)
    z_pad = up(z_rows, 16)

    loads = []
    for i, (src, dst) in enumerate(
        (
            (q_in, q_ref), (k_in, k_ref), (v_in, v_ref), (g_in, g_ref), (w_in, w_ref),
            (len_in, len_ref),
        )
    ):
        loads.append(pltpu.make_async_copy(src, dst, isem.at[i]))
    for c in loads[:3]:
        c.start()

    barrier = pltpu.get_barrier_semaphore()
    for d in far_first(NZ):
        pl.semaphore_signal(
            barrier, inc=1, device_id=(my * NZ + lax.rem(mz + d, NZ), me), device_id_type=MESH
        )
    for d in range(1, NY):
        for x in range(NX):
            other = (lax.rem(my + d, NY) * NZ + mz, 2 * x + me // 4)
            pl.semaphore_signal(barrier, inc=1, device_id=other, device_id_type=MESH)
    for d in range(1, SPREAD):
        pl.semaphore_signal(
            barrier, inc=1, device_id=(dp, lax.rem(me + d, SPREAD)), device_id_type=MESH
        )

    def exchange(kind, send, recv, group=1):
        copies = []
        for d in far_first(SPREAD):
            other = lax.rem(me + d, SPREAD)
            copies.append(
                pltpu.make_async_remote_copy(
                    src_ref=send.at[other // group],
                    dst_ref=recv.at[me],
                    send_sem=ssem.at[kind, d],
                    recv_sem=rsem.at[kind, d],
                    device_id=(dp, other),
                    device_id_type=MESH,
                )
            )
            copies[-1].start()
        return copies

    def arrive(kind, send, recv, group=1):
        for d in range(1, SPREAD):
            source = lax.rem(me + SPREAD - d, SPREAD)
            pltpu.make_async_remote_copy(
                src_ref=send.at[source // group],
                dst_ref=recv.at[source],
                send_sem=ssem.at[kind, d],
                recv_sem=rsem.at[kind, d],
                device_id=(dp, source),
                device_id_type=MESH,
            ).wait_recv()

    def along(size, place, device, send, recv, sem):
        def copy(d, slot, other):
            return pltpu.make_async_remote_copy(
                src_ref=send.at[other],
                dst_ref=recv.at[slot],
                send_sem=sem.at[0, d],
                recv_sem=sem.at[1, d],
                device_id=device(other),
                device_id_type=MESH,
            )

        def start():
            for d in far_first(size):
                copy(d, place, lax.rem(place + d, size)).start()
            recv[place] = send[place]

        def finish():
            for d in range(1, size):
                source = lax.rem(place + size - d, size)
                copy(d, source, source).wait_recv()

        def sent():
            for d in range(1, size):
                copy(d, place, lax.rem(place + d, size)).wait_send()

        return start, finish, sent

    def plane_each(do, own=None, first=None):
        for d in (2, 1, 3, 0):
            y = lax.rem(my + d, NY)
            if first is not None:
                first(y)
            for b in range(NX):
                other = 4 * mc + b
                copy = pltpu.make_async_remote_copy(
                    src_ref=d_send.at[y * NX + b],
                    dst_ref=d_recv.at[d * NX + mx],
                    send_sem=d_sem.at[0, d * NX + b],
                    recv_sem=d_sem.at[1, d * NX + mx],
                    device_id=(y * NZ + mz, other),
                    device_id_type=MESH,
                )
                if d:
                    do(copy)
                else:
                    pl.when(other != me)(functools.partial(do, copy))
                    if own is not None:
                        pl.when(other == me)(functools.partial(own, b))

    def plane_own(b):
        d_recv[mx] = d_send[my * NX + b]

    def plane_arrive():
        for d in (0, 1, 3, 2):
            y = lax.rem(my + NY - d, NY)
            for x in range(NX):
                source = 2 * x + me // 4
                copy = pltpu.make_async_remote_copy(
                    src_ref=d_send.at[0],
                    dst_ref=d_recv.at[d * NX + x],
                    send_sem=d_sem.at[0, d * NX],
                    recv_sem=d_sem.at[1, d * NX + x],
                    device_id=(y * NZ + mz, source),
                    device_id_type=MESH,
                )
                if d:
                    copy.wait_recv()
                else:
                    pl.when(source != me)(copy.wait_recv)

    def total(recv, count):
        out = recv[0].astype(F32)
        for i in range(1, count):
            out = out + recv[i].astype(F32)
        return out

    to = iota((SEG, SEG), 1)
    at = iota((SEG, SEG), 0)
    perm = jnp.where(at == to % CLS * SPREAD + to // CLS, 1.0, 0.0).astype(BF16)
    for i, (src, dst) in enumerate(((q_ref, qt), (k_ref, kt), (v_ref, vt))):
        loads[i].wait()
        if i == 0:
            for c in loads[3:]:
                c.start()
        dst[...] = mm_tn(src[...], perm).astype(BF16).reshape(NHEAD, DH, SEG)
    def class_rows(src, j):
        tile = pl.ds(j // 4 * 128, 128)
        both = jnp.concatenate([src[j, :, tile], src[j + SPREAD, :, tile]], 0)
        return both.astype(F32)

    for j in range(SPREAD):
        send0[j] = pack([class_rows(x, j) for x in (qt, kt, vt)], j, PACK3).astype(BF16)
    recv0[me] = send0[me]
    pl.semaphore_wait(barrier, SPREAD - 1 + (NY - 1) * NX + NZ - 1)
    copies = exchange(0, send0, recv0)

    loads[3].wait()
    ogt[...] = mm_tn(g_ref[...], perm).astype(BF16)
    loads[4].wait()
    dot[...] = mm(w_ref[...], ogt[...]).astype(BF16).reshape(NHEAD, DH, SEG)
    for j in range(SPREAD):
        send1[j] = pack([class_rows(dot, j)], j, PACK1).astype(BF16)
    recv1[me] = send1[me]
    copies += exchange(1, send1, recv1)
    z_at = iota((NZ * z_pad, 128), 0)
    lane = iota((NZ * z_pad, 128), 1)
    z_at = jnp.where(z_at % z_pad < z_rows, z_at // z_pad * z_rows + z_at % z_pad, -1)
    pick_main[...] = jnp.where(lane == z_at, 1.0, 0.0).astype(BF16)
    pick_rest[...] = jnp.where(lane + MAIN == z_at, 1.0, 0.0).astype(BF16)

    loads[5].wait()
    ends = []
    for i in range(SLIDES):
        ends.append(len_ref[0, i] if i == 0 else ends[-1] + len_ref[0, i])
    lane = iota((1, SEG), 1)
    k_mask, q_mask = mask_rows(me * SEG + lane % CLS * SPREAD + lane // CLS, ends)
    row = iota((PAD, SEG), 0)
    ones = jnp.where(row < 2, 1.0, 0.0).astype(BF16)

    def forward_s(h):
        s = scores(qt[h], kt[h], k_mask, q_mask)
        s_all[h] = s
        sta[h, 0:1] = jnp.max(s, 0, keepdims=True)

    def forward_o(h):
        e, o, top, lse = weigh(s_all[h], sta[h, 0:1], vt[h], ones)
        e_all[h] = e
        ot[h] = o
        att[pl.ds(pl.multiple_of(h * DH, 16), DH)] = o.astype(BF16)
        sta[h, 0:1] = top
        sta[h, 1:2] = lse
        sta[h, 2:3] = jnp.sum(dot[h].astype(F32) * o, 0, keepdims=True)

    def loop(body, first, last, unroll):
        def step(i, carry):
            for u in range(unroll):
                body(i * unroll + u)
            return carry

        lax.fori_loop(first // unroll, last // unroll, step, 0)

    loop(forward_s, 0, NHEAD, UF)
    loop(forward_o, 0, NHEAD, UF)

    lse_own[...] = sta[:, 1, :]
    early = [
        (att, att_x),
        (lse_own, lse_x),
        (ogt.at[pl.ds(pl.multiple_of((1 - mc) * COLH, 128), COLH)], og_x),
    ]
    sibling = [
        pltpu.make_async_remote_copy(
            src_ref=src,
            dst_ref=dst,
            send_sem=c_sem.at[0, i],
            recv_sem=c_sem.at[1, i],
            device_id=(dp, 2 * mx + 1 - mc),
            device_id_type=MESH,
        )
        for i, (src, dst) in enumerate(early)
    ]
    for c in sibling:
        c.start()

    narrow = lane_block(8)
    for j in range(SPREAD):
        tile = pl.ds(j // 4 * 128, 128)
        rows = jnp.concatenate(
            [sta[j, 1:2, tile], sta[j + SPREAD, 1:2, tile],
             sta[j, 2:3, tile], sta[j + SPREAD, 2:3, tile],
             jnp.zeros((4, 128), F32)], 0)
        send2[j] = shift(rows, -j)
    recv2[me] = send2[me]
    copies += exchange(2, send2, recv2)

    block = lane_block(PAIR)

    def gather(recv, dsts):
        for half in range(2):
            tile = pl.ds(half * 128, 128)
            outs = [jnp.zeros((PAIR, 128), F32)] * len(dsts)
            for s in range(half * 4, half * 4 + 4):
                got = recv[s].astype(F32)
                for t in range(len(dsts)):
                    outs[t] = jnp.where(block == s % 4, unpack(got, t, s), outs[t])
            for dst, out in zip(dsts, outs):
                out = out.astype(BF16)
                for u in range(2):
                    dst[u, :, tile] = out[u * DH : (u + 1) * DH]

    arrive(0, send0, recv0)
    gather(recv0, (qb, kb, vb))
    kb_mask, qb_mask = mask_rows(lane * SPREAD + me, ends)
    for u in range(2):
        e, o, top, lse = forward_head(qb[u], kb[u], vb[u], kb_mask, qb_mask, ones)
        eb[u] = e
        ob[u] = o
        sb[u, 0:1] = top
        sb[u, 1:2] = lse
    for s in range(SPREAD):
        tile = pl.ds(s // 4 * 128, 128)
        both = jnp.concatenate([ob[0, :, tile], ob[1, :, tile]], 0)
        lses = jnp.where(
            lane_block(1) == 0, shift(sb[0, 1:2, tile], -s), shift(sb[1, 1:2, tile], 1 - s)
        )
        dense = jnp.concatenate([pack([both], s, DENSE), three_terms(lses)], 0)
        send3[s // 2, s % 2] = dense.astype(BF16)
    recv3[me] = send3[mx]
    copies += exchange(3, send3, recv3, 2)
    arrive(1, send1, recv1)
    gather(recv1, (db,))
    for u in range(2):
        sb[u, 2:3] = jnp.sum(db[u].astype(F32) * ob[u], 0, keepdims=True)
    for s in range(SPREAD):
        tile = pl.ds(s // 4 * 128, 128)
        rows = jnp.concatenate([sb[0, 2:3, tile], sb[1, 2:3, tile], jnp.zeros((6, 128), F32)], 0)
        send4[s] = shift(rows, -s)
    recv4[me] = send4[me]
    copies += exchange(4, send4, recv4)

    tall = iota((NHEAD, 128), 0)
    spot = lane_block(NHEAD)

    def spread_rows(pairs, empty):
        sides = []
        for half in range(2):
            out = jnp.full((NHEAD, 128), empty, F32)
            for j in range(half * 4, half * 4 + 4):
                for u in range(2):
                    here = (tall == j + SPREAD * u) & (spot == j % 4)
                    out = jnp.where(here, pairs[j][u], out)
            sides.append(out)
        return jnp.concatenate(sides, 1)

    def combine(which, lse_a, target):
        got = [recv3[j, which].astype(F32) for j in range(SPREAD)]
        pairs = []
        for j in range(SPREAD):
            x = got[j][DENSE : DENSE + 1] + got[j][DENSE + 1 : DENSE + 2]
            x = x + got[j][DENSE + 2 : DENSE + 3]
            pairs.append((shift(x, j), shift(x, j - 1)))
        lse, w_a, w_b = blend(lse_a, spread_rows(pairs, -1e30))
        for j in range(SPREAD):
            other = unpack(got[j], 0, j)
            tile = slice(j // 4 * 128, j // 4 * 128 + 128)
            for u in range(2):
                h = j + SPREAD * u
                mine = target[h * DH : (h + 1) * DH, tile].astype(F32)
                both = mine * w_a[h : h + 1, tile]
                both = both + other[u * DH : (u + 1) * DH] * w_b[h : h + 1, tile]
                x = jnp.where(lane_block(DH) == j % 4, both, mine)
                target[h * DH : (h + 1) * DH, tile] = x.astype(BF16)
        return lse, w_a, w_b

    for c in sibling:
        c.wait()
    arrive(3, send3, recv3, 2)
    lse, w_a, w_b = combine(mc, lse_own[...], att)
    combine(1 - mc, lse_x[...], att_x)

    zz = along(NZ, mz, lambda z: (my * NZ + z, me), z_send, z_recv, z_sem)
    def block_of(y):
        rows = pl.ds(pl.multiple_of(y * (MAIN + REM), REM), MAIN + REM)
        cols = pl.ds(pl.multiple_of(mc * COLH, 128), COLH)
        out = mm_nt(ogt[cols], att[rows]) + mm_nt(og_x[...], att_x[rows])
        for b in range(NX):
            x = out[b * COLS : (b + 1) * COLS]
            rest = jnp.concatenate([x[: COLS // 2, MAIN:], x[COLS // 2 :, MAIN:]], 1)
            d_send[y * NX + b, :COLS] = x[:, :MAIN].astype(BF16)
            d_send[y * NX + b, COLS:] = rest.astype(BF16)

    plane_each(lambda copy: copy.start(), plane_own, block_of)

    arrive(4, send4, recv4)
    pairs = []
    for j in range(SPREAD):
        x = shift(recv4[j], j)
        pairs.append((x[0:1], x[1:2]))
    sta[:, 2, :] = w_a * sta[:, 2, :] + w_b * spread_rows(pairs, 0.0)
    sta[:, 3, :] = jnp.exp2(sta[:, 0, :] - lse)

    def step_z():
        plane_arrive()
        x = total(d_recv, NY * NX)
        rest = jnp.concatenate([x[COLS:], pltpu.roll(x[COLS:], REM, 1)], 0)
        pad = jnp.zeros((128 - COLS, 128), F32)
        x = jnp.concatenate([x[:COLS], pad], 0).astype(BF16)
        rest = jnp.concatenate([rest, pad], 0).astype(BF16)
        x = (mm_nt(pick_main[...], x) + mm_nt(pick_rest[...], rest)).astype(BF16)
        for z in range(NZ):
            z_send[z] = x[z * z_pad : (z + 1) * z_pad]
        zz[0]()

    def finish():
        zz[1]()
        dw_ref[...] = total(z_recv, NZ)

    arrive(2, send2, recv2)
    halves = []
    for half in range(2):
        out = jnp.zeros((8, 128), F32)
        for s in range(half * 4, half * 4 + 4):
            out = jnp.where(narrow == s % 4, shift(recv2[s], s), out)
        halves.append(out)
    theirs = jnp.concatenate(halves, 1)
    for u in range(2):
        top = sb[u, 0:1]
        lse, w_a, w_b = blend(theirs[u : u + 1], sb[u, 1:2])
        delta = w_a * theirs[2 + u : 3 + u] + w_b * sb[u, 2:3]
        grads_b = backward_head(
            qb[u], kb[u], vb[u], db[u], eb[u], ones, jnp.exp2(top - lse), delta
        )
        for t in range(3):
            gb[t, u * DH : (u + 1) * DH] = grads_b[t]
    for s in range(SPREAD):
        tile = pl.ds(s // 4 * 128, 128)
        send5[s] = pack([gb[t, :, tile] for t in range(3)], s, PACK3).astype(BF16)
    recv5[me] = send5[me]

    def backward(h):
        dq, dk, dv = backward_head(
            qt[h], kt[h], vt[h], dot[h], e_all[h], ones, sta[h, 3:4], sta[h, 2:3]
        )
        dqt[h] = dq
        dkt[h] = dk
        dvt[h] = dv

    copies += exchange(5, send5, recv5)
    loop(backward, 0, NHEAD, UB)
    step_z()

    arrive(5, send5, recv5)
    for j in range(SPREAD):
        tile = pl.ds(j // 4 * 128, 128)
        got = recv5[j].astype(F32)
        for t, dst in enumerate((dqt, dkt, dvt)):
            part = jnp.where(block == j % 4, unpack(got, t, j), 0.0)
            for u in range(2):
                h = j + SPREAD * u
                dst[h, :, tile] = dst[h, :, tile] + part[u * DH : (u + 1) * DH]
    stores = []
    for t, src in enumerate((dqt, dkt, dvt)):
        grads[t] = mm_nt(perm, src[...].reshape(D, SEG).astype(BF16)).astype(BF16)
        stores.append(pltpu.make_async_copy(grads.at[t], grads_ref.at[t], osem.at[t]))
        stores[-1].start()

    finish()
    for c in stores:
        c.wait()
    for c in copies:
        c.wait_send()
    plane_each(lambda copy: copy.wait_send())
    zz[2]()


def final_kernel(grads_ref, part_ref, dq_ref, dk_ref, dv_ref, dw_ref, x, part, dw, isem, osem):
    loads = [pltpu.make_async_copy(grads_ref.at[t], x.at[t], isem.at[t]) for t in range(3)]
    loads.append(pltpu.make_async_copy(part_ref, part, isem.at[3]))
    for c in loads:
        c.start()
    stores = []
    for t, dst in enumerate((dq_ref, dk_ref, dv_ref)):
        loads[t].wait()
        stores.append(pltpu.make_async_copy(x.at[t], dst, osem.at[t]))
        stores[-1].start()
    loads[3].wait()
    dw[...] = part[0 : dw.shape[0], 0 : dw.shape[1]]
    stores.append(pltpu.make_async_copy(dw, dw_ref, osem.at[3]))
    stores[-1].start()
    for c in stores:
        c.wait()


def on_device(queries, keys, values, out_grad, out_weight, slide_lengths):
    vmem = pl.BlockSpec(memory_space=pltpu.VMEM)
    heads = lambda n, dtype: pltpu.VMEM((n, DH, SEG), dtype)
    z_rows = D // (NY * NZ)
    z_pad = up(z_rows, 16)
    grads, partial = pl.pallas_call(
        kernel,
        out_shape=(
            jax.ShapeDtypeStruct((3, SEG, D), BF16),
            jax.ShapeDtypeStruct((z_pad, 128), F32),
        ),
        in_specs=[pl.BlockSpec(memory_space=pl.ANY)] * 6,
        out_specs=(pl.BlockSpec(memory_space=pl.ANY), vmem),
        scratch_shapes=[
            pltpu.VMEM((SEG, D), BF16), pltpu.VMEM((SEG, D), BF16), pltpu.VMEM((SEG, D), BF16),
            pltpu.VMEM((SEG, D), BF16), pltpu.VMEM((D, D), BF16),
            pltpu.SMEM((1, SLIDES), jnp.int32),
            pltpu.SemaphoreType.DMA((6,)),
            pltpu.VMEM((3, SEG, D), BF16),
            pltpu.SemaphoreType.DMA((3,)),
            heads(NHEAD, BF16), heads(NHEAD, BF16), heads(NHEAD, BF16), heads(NHEAD, BF16),
            pltpu.VMEM((NHEAD, SEG, SEG), F32),
            pltpu.VMEM((NHEAD, SEG, SEG), BF16),
            heads(NHEAD, F32),
            pltpu.VMEM((NHEAD, 8, SEG), F32),
            pltpu.VMEM((D, SEG), BF16),
            heads(NHEAD, F32), heads(NHEAD, F32), heads(NHEAD, F32),
            heads(2, BF16), heads(2, BF16), heads(2, BF16), heads(2, BF16),
            pltpu.VMEM((2, SEG, SEG), BF16),
            heads(2, F32),
            pltpu.VMEM((2, 8, SEG), F32),
            pltpu.VMEM((3, PAIR, SEG), F32),
            pltpu.VMEM((SPREAD, PACK3, 128), BF16), pltpu.VMEM((SPREAD, PACK3, 128), BF16),
            pltpu.VMEM((SPREAD, PACK1, 128), BF16), pltpu.VMEM((SPREAD, PACK1, 128), BF16),
            pltpu.VMEM((SPREAD, 8, 128), F32), pltpu.VMEM((SPREAD, 8, 128), F32),
            pltpu.VMEM((SPREAD // 2, 2, PACK1, 128), BF16),
            pltpu.VMEM((SPREAD, 2, PACK1, 128), BF16),
            pltpu.VMEM((SPREAD, 8, 128), F32), pltpu.VMEM((SPREAD, 8, 128), F32),
            pltpu.VMEM((SPREAD, PACK3, 128), BF16), pltpu.VMEM((SPREAD, PACK3, 128), BF16),
            pltpu.SemaphoreType.DMA((6, SPREAD)),
            pltpu.SemaphoreType.DMA((6, SPREAD)),
            pltpu.VMEM((NZ * z_pad, 128), BF16), pltpu.VMEM((NZ * z_pad, 128), BF16),
            pltpu.VMEM((D, SEG), BF16),
            pltpu.VMEM((D, SEG), BF16),
            pltpu.VMEM((NHEAD, SEG), F32), pltpu.VMEM((NHEAD, SEG), F32),
            pltpu.VMEM((COLH, SEG), BF16),
            pltpu.VMEM((NY * NX, DROWS, 128), BF16), pltpu.VMEM((NY * NX, DROWS, 128), BF16),
            pltpu.VMEM((NZ, z_pad, 128), BF16), pltpu.VMEM((NZ, z_pad, 128), BF16),
            pltpu.SemaphoreType.DMA((2, 3)),
            pltpu.SemaphoreType.DMA((2, NY * NX)),
            pltpu.SemaphoreType.DMA((2, NZ)),
        ],
        compiler_params=pltpu.CompilerParams(
            collective_id=0, has_side_effects=True, vmem_limit_bytes=VMEM_LIMIT
        ),
    )(queries, keys, values, out_grad, out_weight, slide_lengths)
    out = jax.ShapeDtypeStruct((SEG, D), BF16)
    return pl.pallas_call(
        final_kernel,
        out_shape=(out, out, out, jax.ShapeDtypeStruct((z_rows, COLS), F32)),
        in_specs=[pl.BlockSpec(memory_space=pl.ANY)] * 2,
        out_specs=(pl.BlockSpec(memory_space=pl.ANY),) * 4,
        scratch_shapes=[
            pltpu.VMEM((3, SEG, D), BF16),
            pltpu.VMEM((z_pad, 128), F32),
            pltpu.VMEM((z_rows, COLS), F32),
            pltpu.SemaphoreType.DMA((4,)),
            pltpu.SemaphoreType.DMA((4,)),
        ],
        compiler_params=pltpu.CompilerParams(vmem_limit_bytes=VMEM_LIMIT),
    )(grads, partial)


def solution(mesh):
    placed = (
        P(("dp", "seq"), None),
        P(("dp", "seq"), None),
        P(("dp", "seq"), None),
        P(("dp", "seq"), None),
        P(),
        P("dp", None),
    )
    return jax.shard_map(
        on_device,
        mesh=mesh,
        in_specs=placed,
        out_specs=(
            P(("dp", "seq"), None),
            P(("dp", "seq"), None),
            P(("dp", "seq"), None),
            P("dp", "seq"),
        ),
        check_vma=False,
    )
```
